32 devices in a mesh: row: 8 (over y, x, core), col: 4 (over z).
Axes of the slice: x: 2, y: 2, z: 4, core: 2. Of those that a mesh axis runs over, the one named last changes fastest.
Arguments:
- matrix: float32 [8192, 2048], P('row', 'col'), may hold values from -100 to 100, as said below
Outputs:
- updated: float32 [8192, 2048], P('row', 'col')
- top: float32 [128, 2048], P(None, 'col')
The draws below stay inside these ranges and needn't reach their ends.
Inputs may be any that keep to these rules, and one draw needn't show every extreme that they name: The first 128 columns of matrix have full column rank.
All inputs are finite; a program needn't handle non-finite values.
Results may differ from the reference program's by a relative error of at most 0.0006.
Values sent between devices are 32-bit elements; how exact they have to be, the bound alone decides.
A program may use at most 64 MiB of HBM per device.

```python
import math
import jax
import jax.numpy as jnp
from jax import lax

B = 128
ROWS = 8192
COLS = 2048


def draw_matrix(key, part):
    key_base = jax.random.fold_in(key, 0)
    key_rows = jax.random.fold_in(key, 1)
    key_cols = jax.random.fold_in(key, 2)
    key_left = jax.random.fold_in(key, 4)
    key_right = jax.random.fold_in(key, 5)
    rise = 1.0 + 2.0 * jnp.arange(ROWS, dtype=jnp.float32)[:, None] / ROWS
    col_scale = jnp.exp(jax.random.uniform(key_cols, (1, COLS), jnp.float32, 0.0, math.log(4.0)))
    noise = jnp.clip(jax.random.normal(key_base, (ROWS, COLS), jnp.float32), -6.0, 6.0)
    base = noise
    row_scale = jnp.exp(jax.random.uniform(key_rows, (ROWS, 1), jnp.float32, 0.0, math.log(4.0)))
    left = jnp.clip(jax.random.normal(key_left, (ROWS, 4), jnp.float32), -2.5, 2.5)
    right = jnp.clip(jax.random.normal(key_right, (4, COLS), jnp.float32), -2.5, 2.5)
    shared = left[:, 0:1] * right[0:1, :] + left[:, 1:2] * right[1:2, :]
    shared = shared + left[:, 2:3] * right[2:3, :] + left[:, 3:4] * right[3:4, :]
    near = 0.125 * shared + 0.0025 * noise
    in_panel = jnp.arange(COLS)[None, :] < B
    mixed = jnp.where(in_panel, near, base)
    return 0.25 * mixed * row_scale * col_scale * rise


def setup_inputs(seed: int = 0) -> dict:
    arg_keys = jax.random.split(jax.random.key(seed), 2)
    matrix = draw_matrix(jax.random.fold_in(arg_keys[1], 71), 0)
    return dict(matrix=matrix)


def matmul(left, right):
    return jnp.dot(left.astype(jnp.float32), right.astype(jnp.float32), precision=lax.Precision.HIGHEST, preferred_element_type=jnp.float32)

def project(left, right):
    return jnp.einsum('rb,rc->bc', left, right, precision=lax.Precision.HIGHEST)

def factor_once(block, gram_mat):
    lower = jnp.linalg.cholesky(gram_mat)
    identity = jnp.eye(block.shape[1], dtype=jnp.float32)
    inverse = jax.scipy.linalg.solve_triangular(lower, identity, lower=True)
    return (matmul(block, inverse.T), lower.T)

def factor_twice(block):
    first_q, first_r = factor_once(block, project(block, block))
    second_q, second_r = factor_once(first_q, project(first_q, first_q))
    return (second_q, matmul(second_r, first_r))

def reference(matrix):
    panel = matrix[:, :B]
    basis, upper = factor_twice(panel)
    coeffs = project(basis, matrix)
    updated = matrix - matmul(basis, coeffs)
    scale = math.sqrt(ROWS)
    updated = jnp.concatenate([basis * scale, updated[:, B:]], 1)
    return (updated, coeffs / scale)
```

```python
import functools
import math

import jax
import jax.numpy as jnp
from jax import lax
from jax.experimental import pallas as pl
from jax.experimental.pallas import tpu as pltpu
from jax.sharding import PartitionSpec as P

B = 128
S = 8
CHUNKS = 8
HI = lax.Precision.HIGHEST


def mm(left, right, dims):
    return lax.dot_general(
        left, right, (dims, ((), ())), precision=HI, preferred_element_type=jnp.float32
    )


def factor_steps(w_ref, low, high, state=None, after_step=None):
    lane = lax.broadcasted_iota(jnp.int32, (S, B), 1)
    sub = lax.broadcasted_iota(jnp.int32, (S, B), 0)
    wide = lax.broadcasted_iota(jnp.int32, (B - 2 * S, B), 1)

    def step(k, state):
        rows, mult, last = state
        d = {}
        for j in range(S):
            column = jnp.broadcast_to(rows[:, j : j + 1], (S, B))
            for i in range(j, S):
                d[i, j] = jnp.broadcast_to(column[i : i + 1], (S, B))
        rest = w_ref[S : B - S] - mm(mult, last, ((0,), (0,)))[2 * S :]
        rest = pltpu.roll(jnp.where(wide < S, 0.0, rest), B - S, 1)
        w_ref[: B - 2 * S] = rest
        w_ref[B - 2 * S : B - S] = pltpu.roll(jnp.where(lane < S, 0.0, last), B - S, 1)
        rows = jnp.where(lane < S, jnp.where(lane == sub, 1.0, 0.0), rows)
        p = [jnp.broadcast_to(rows[j : j + 1], (S, B)) for j in range(S)]
        t = None
        for j in range(S):
            inv = lax.rsqrt(d[j, j])
            l = {i: d[i, j] * inv for i in range(j + 1, S)}
            for i in range(j + 1, S):
                for m in range(j + 1, i + 1):
                    d[i, m] = d[i, m] - l[i] * l[m]
            tj = p[j] * inv
            for i in range(j + 1, S):
                p[i] = p[i] - l[i] * tj
            t = tj if t is None else jnp.where(sub == j, tj, t)
        mult = jnp.where((lane >= S) & (lane < B - S * k), t, 0.0)
        last = pltpu.roll(t, B - S, 1)
        after = rest[:S]
        for i in range(S):
            column = jnp.broadcast_to(mult[:, S + i : S + i + 1], (S, B))
            drop = jnp.sum(column * last, axis=0, keepdims=True)
            after = jnp.where(sub == i, after - drop, after)
        if after_step is not None:
            after_step(k)
        return after, mult, last

    if low == 0:
        state = (w_ref[:S], jnp.zeros((S, B), jnp.float32), w_ref[B - S :])
    state = lax.fori_loop(low, high, step, state)
    if high == B // S:
        w_ref[B - S :] = state[2]
    return state


class Sum:
    def __init__(self, size, me, src, box, full, sems):
        self.size, self.me, self.src, self.box, self.full = size, me, src, box, full
        self.sems = sems
        self.slab = max(8, B // size)
        self.owners = B // self.slab

    def rows(self, owner):
        return pl.ds(pl.multiple_of(owner * self.slab, self.slab), self.slab)

    def own(self, device, what):
        if self.owners == self.size:
            what()
        else:
            pl.when(device < self.owners)(what)

    def scatter_copy(self, i):
        peer = self.me ^ i
        return pltpu.make_async_remote_copy(
            src_ref=self.src.at[self.rows(peer)],
            dst_ref=self.box.at[i],
            send_sem=self.sems.at[0, i],
            recv_sem=self.sems.at[1, i],
            device_id={"row": peer},
            device_id_type=pl.DeviceIdType.MESH,
        )

    def scatter_from(self, i):
        return pltpu.make_async_remote_copy(
            src_ref=self.box.at[i],
            dst_ref=self.box.at[i],
            send_sem=self.sems.at[0, i],
            recv_sem=self.sems.at[1, i],
            device_id={"row": self.me ^ i},
            device_id_type=pl.DeviceIdType.MESH,
        )

    def gather_copy(self, i, owner):
        return pltpu.make_async_remote_copy(
            src_ref=self.full.at[self.rows(owner)],
            dst_ref=self.full.at[self.rows(owner)],
            send_sem=self.sems.at[2, i],
            recv_sem=self.sems.at[3, i],
            device_id={"row": self.me ^ i},
            device_id_type=pl.DeviceIdType.MESH,
        )

    def start(self):
        for i in range(1, self.size):
            self.own(self.me ^ i, lambda: self.scatter_copy(i).start())

    def middle(self):
        for i in range(1, self.size):
            self.own(self.me ^ i, lambda: self.scatter_copy(i).wait_send())

        def add():
            total = self.src[self.rows(self.me)]
            for i in range(1, self.size):
                self.scatter_from(i).wait_recv()
                total = total + self.box[i]
            self.full[self.rows(self.me)] = total
            self.box[0] = total

        self.own(self.me, add)

    def spread(self):
        def send():
            for i in range(1, self.size):
                self.gather_copy(i, self.me).start()

        self.own(self.me, send)

    def end(self):
        for i in range(1, self.size):
            self.own(self.me ^ i, lambda: self.gather_copy(i, self.me ^ i).wait_recv())

    def drain(self):
        def sent():
            for i in range(1, self.size):
                self.gather_copy(i, self.me).wait_send()

        self.own(self.me, sent)


def kernel(
    nrow, ncol, m_hbm, m_v, q_v, g2_v, p_v,
    a_v, s1_v, s2_v, sp_v, g1_v, box1, box2, boxp,
    in_sems, chain_sems, g_sems, sems1, sems2, semsp,
):
    me = lax.axis_index("row")
    z = lax.axis_index("col")
    height = m_v.shape[0]
    part = height // CHUNKS
    load_m = pltpu.make_async_copy(m_hbm, m_v, in_sems.at[0])
    load_a = pltpu.make_async_copy(m_hbm.at[:, pl.ds(0, B)], a_v, in_sems.at[1])

    barrier = pltpu.get_barrier_semaphore()
    for i in range(1, nrow):
        pl.semaphore_signal(
            barrier, inc=1, device_id={"row": me ^ i}, device_id_type=pl.DeviceIdType.MESH
        )
    for i in range(1, ncol):
        pl.semaphore_signal(
            barrier, inc=1, device_id={"col": z ^ i}, device_id_type=pl.DeviceIdType.MESH
        )

    pl.when(z == 0)(load_a.start)
    load_m.start()
    pl.semaphore_wait(barrier, nrow + ncol - 2)

    def chain(c):
        block = a_v.at[pl.ds(pl.multiple_of(c * part, part), part)]
        return pltpu.make_async_remote_copy(
            src_ref=block,
            dst_ref=block,
            send_sem=chain_sems.at[0, c],
            recv_sem=chain_sems.at[1, c],
            device_id={"col": lax.rem(z + 1, ncol)},
            device_id_type=pl.DeviceIdType.MESH,
        )

    passes_on = (z > 0) & (z < ncol - 1)

    def forward(c):
        chain(c).wait_recv()
        chain(c).start()

    first = Sum(nrow, me, s1_v, box1, g1_v, sems1)
    second = Sum(nrow, me, s2_v, box2, g2_v, sems2)
    coeffs = Sum(nrow, me, sp_v, boxp, p_v, semsp)

    def hand(which, total, i):
        return pltpu.make_async_remote_copy(
            src_ref=total.box.at[0],
            dst_ref=total.full.at[total.rows(me)],
            send_sem=g_sems.at[2 * which, i],
            recv_sem=g_sems.at[2 * which + 1, 0],
            device_id={"col": i},
            device_id_type=pl.DeviceIdType.MESH,
        )

    def give(which, total):
        def send():
            for i in range(1, ncol):
                hand(which, total, i).start()

        first.own(me, send)

    @pl.when(z == 0)
    def _():
        load_a.wait()
        for c in range(3):
            chain(c).start()
        s1_v[...] = mm(a_v[...], a_v[...], ((0,), (0,)))
        first.start()
        first.middle()
        give(0, first)
        first.spread()
        for c in range(3, CHUNKS):
            chain(c).start()

    @pl.when(passes_on)
    def _():
        for c in range(4):
            forward(c)

    @pl.when(z > 0)
    def _():
        first.own(me, lambda: hand(0, first, 0).wait_recv())
        first.spread()

    first.end()
    first.drain()

    def pass_on(k):
        @pl.when(passes_on & (k % 3 == 1) & (k < 12))
        def _():
            forward(4 + k // 3)

    factor_steps(g1_v, 0, B // S, None, pass_on)

    big = 2 * part

    @pl.when(z == 0)
    def _():
        for c in range(CHUNKS // 2):
            rows = pl.ds(c * big, big)
            q_v[rows] = mm(a_v[rows], g1_v[...], ((1,), (1,)))
        q = q_v[...]
        s2_v[...] = mm(q, q, ((0,), (0,)))
        second.start()
        load_m.wait()
        sp_v[...] = mm(q_v[...], m_v[...], ((0,), (0,)))
        second.middle()
        give(1, second)
        second.spread()
        coeffs.start()

    @pl.when(z > 0)
    def _():
        load_m.wait()
        for c in range(CHUNKS // 2):
            if c == CHUNKS // 2 - 1:
                second.own(me, lambda: hand(1, second, 0).wait_recv())
                second.spread()

            @pl.when(z == ncol - 1)
            def _():
                chain(2 * c).wait_recv()
                chain(2 * c + 1).wait_recv()

            rows = pl.ds(c * big, big)
            q = mm(a_v[rows], g1_v[...], ((1,), (1,)))
            q_v[rows] = q
            term = mm(q, m_v[rows], ((0,), (0,)))
            if c == 0:
                sp_v[...] = term
            else:
                sp_v[...] += term
        coeffs.start()

    second.end()
    second.drain()
    state = factor_steps(g2_v, 0, B // S // 2)
    coeffs.middle()
    coeffs.spread()
    factor_steps(g2_v, B // S // 2, B // S, state)
    coeffs.end()
    coeffs.drain()

    @pl.when(z == 0)
    def _():
        def given():
            for i in range(1, ncol):
                hand(0, first, i).wait_send()
                hand(1, second, i).wait_send()

        first.own(me, given)

    @pl.when(z < ncol - 1)
    def _():
        for c in range(CHUNKS):
            chain(c).wait_send()


def halves(x):
    high = x.astype(jnp.bfloat16)
    return high, (x - high.astype(jnp.float32)).astype(jnp.bfloat16)


def project_kernel(rows, m_ref, q_ref, g2_ref, p_ref, out_hbm, top_ref, out_v, back_v, sems):
    height, width = m_ref.shape
    part = height // 4
    scale = math.sqrt(rows)
    on_panel = lax.axis_index("col") == 0
    g2 = g2_ref[...]
    c = mm(g2, p_ref[...], ((1,), (0,)))
    top_ref[...] = c / scale
    back = mm(g2, c, ((0,), (0,)))
    leading = jnp.where(on_panel, -scale * g2.T, back[:, :B])
    high, low = halves(jnp.concatenate([leading, back[:, B:]], 1))
    back_v[:B] = high
    back_v[B : 2 * B] = high
    back_v[2 * B :] = low

    def store(i):
        block = pl.ds(i * part, part)
        return pltpu.make_async_copy(out_v.at[block], out_hbm.at[block], sems.at[i])

    for i in range(4):
        block = pl.ds(i * part, part)
        high, low = halves(q_ref[block])
        change = jnp.dot(
            jnp.concatenate([high, low, high], 1), back_v[...], preferred_element_type=jnp.float32
        )
        base = m_ref[block]
        out_v[block, :B] = jnp.where(on_panel, 0.0, base[:, :B]) - change[:, :B]
        out_v[block, B:] = base[:, B:] - change[:, B:]
        store(i).start()
    for i in range(4):
        store(i).wait()


def on_device(nrow, ncol, matrix):
    height, width = matrix.shape
    slab = max(8, B // nrow)
    f32 = jnp.float32
    dma = pltpu.SemaphoreType.DMA
    shape = jax.ShapeDtypeStruct
    held, basis, inverse, coeffs = pl.pallas_call(
        functools.partial(kernel, nrow, ncol),
        out_shape=(
            shape((height, width), f32), shape((height, B), f32), shape((B, B), f32), shape((B, width), f32)
        ),
        in_specs=[pl.BlockSpec(memory_space=pltpu.HBM)],
        out_specs=(pl.BlockSpec(memory_space=pltpu.VMEM),) * 4,
        scratch_shapes=[
            pltpu.VMEM((height, B), f32),
            pltpu.VMEM((B, B), f32),
            pltpu.VMEM((B, B), f32),
            pltpu.VMEM((B, width), f32),
            pltpu.VMEM((B, B), f32),
            pltpu.VMEM((nrow, slab, B), f32),
            pltpu.VMEM((nrow, slab, B), f32),
            pltpu.VMEM((nrow, slab, width), f32),
            dma((2,)),
            dma((2, CHUNKS)),
            dma((4, ncol)),
            dma((4, nrow)),
            dma((4, nrow)),
            dma((4, nrow)),
        ],
        compiler_params=pltpu.CompilerParams(
            collective_id=0, has_side_effects=True, vmem_limit_bytes=12 * 2**20
        ),
    )(pltpu.with_memory_space_constraint(matrix, pltpu.HBM))
    whole = pl.BlockSpec(memory_space=pltpu.VMEM)
    return pl.pallas_call(
        functools.partial(project_kernel, height * nrow),
        out_shape=(shape((height, width), f32), shape((B, width), f32)),
        in_specs=[whole] * 4,
        out_specs=(pl.BlockSpec(memory_space=pl.ANY), whole),
        scratch_shapes=[
            pltpu.VMEM((height, width), f32),
            pltpu.VMEM((3 * B, width), jnp.bfloat16),
            dma((4,)),
        ],
        compiler_params=pltpu.CompilerParams(vmem_limit_bytes=12 * 2**20),
    )(held, basis, inverse, coeffs)


def solution(mesh):
    nrow, ncol = mesh.shape["row"], mesh.shape["col"]
    return jax.shard_map(
        functools.partial(on_device, nrow, ncol),
        mesh=mesh,
        in_specs=(P("row", "col"),),
        out_specs=(P("row", "col"), P(None, "col")),
        check_vma=False,
    )
```

```python
import functools
import math

import jax
import jax.numpy as jnp
from jax import lax
from jax.experimental import pallas as pl
from jax.experimental.pallas import tpu as pltpu
from jax.sharding import PartitionSpec as P

B = 128
S = 8
CHUNKS = 8
HI = lax.Precision.HIGHEST


def mm(left, right, dims):
    return lax.dot_general(
        left, right, (dims, ((), ())), precision=HI, preferred_element_type=jnp.float32
    )


def thirds(x):
    high = x.astype(jnp.bfloat16).astype(jnp.float32)
    rest = x - high
    mid = rest.astype(jnp.bfloat16).astype(jnp.float32)
    return high, mid, rest - mid


def self_product(t):
    high, mid, low = thirds(t)
    left = jnp.concatenate([high, high, mid, mid, high, low], 0).astype(jnp.bfloat16)
    right = jnp.concatenate([high, mid, high, mid, low, high], 0).astype(jnp.bfloat16)
    return lax.dot_general(
        left, right, (((0,), (0,)), ((), ())), preferred_element_type=jnp.float32
    )


def factor_steps(w_ref, c_ref, low, high, state=None, after_step=None):
    lane = lax.broadcasted_iota(jnp.int32, (S, B), 1)
    sub = lax.broadcasted_iota(jnp.int32, (S, B), 0)
    count = B // S
    w = [w_ref[S * r : S * r + S] for r in range(count)] if state is None else state
    for k in range(low, high):
        here = (lane >= S * k) & (lane < S * k + S)
        rows = w[k]
        d = {}
        for j in range(S):
            c_ref[S * j : S * j + S] = jnp.broadcast_to(
                rows[:, S * k + j : S * k + j + 1], (S, B)
            )
            for i in range(j, S):
                d[i, j] = jnp.broadcast_to(c_ref[S * j + i : S * j + i + 1], (S, B))
        rows = jnp.where(here, jnp.where(lane - S * k == sub, 1.0, 0.0), rows)
        p = [jnp.broadcast_to(rows[j : j + 1], (S, B)) for j in range(S)]
        t = None
        for j in range(S):
            inv = lax.rsqrt(d[j, j])
            l = {i: d[i, j] * inv for i in range(j + 1, S)}
            for i in range(j + 1, S):
                for m in range(j + 1, i + 1):
                    d[i, m] = d[i, m] - l[i] * l[m]
            tj = p[j] * inv
            for i in range(j + 1, S):
                p[i] = p[i] - l[i] * tj
            t = tj if t is None else jnp.where(sub == j, tj, t)
        w_ref[S * k : S * k + S] = jnp.where(lane < S * k + S, t, 0.0)
        if k + 1 < count:
            after = jnp.where(here, 0.0, w[k + 1])
            for i in range(S):
                at = S * (k + 1) + i
                column = jnp.broadcast_to(t[:, at : at + 1], (S, B))
                drop = jnp.sum(column * t, axis=0, keepdims=True)
                after = jnp.where(sub == i, after - drop, after)
            w[k + 1] = after
        if k + 2 < count:
            change = self_product(t)
            for r in range(k + 2, count):
                w[r] = jnp.where(here, 0.0, w[r]) - change[S * r : S * r + S]
        if after_step is not None:
            after_step(k)
    return w


class Sum:
    def __init__(self, size, me, src, box, full, sems):
        self.size, self.me, self.src, self.box, self.full = size, me, src, box, full
        self.sems = sems
        self.slab = max(8, B // size)
        self.owners = B // self.slab

    def rows(self, owner):
        return pl.ds(pl.multiple_of(owner * self.slab, self.slab), self.slab)

    def own(self, device, what):
        if self.owners == self.size:
            what()
        else:
            pl.when(device < self.owners)(what)

    def scatter_copy(self, i):
        peer = self.me ^ i
        return pltpu.make_async_remote_copy(
            src_ref=self.src.at[self.rows(peer)],
            dst_ref=self.box.at[i],
            send_sem=self.sems.at[0, i],
            recv_sem=self.sems.at[1, i],
            device_id={"row": peer},
            device_id_type=pl.DeviceIdType.MESH,
        )

    def scatter_from(self, i):
        return pltpu.make_async_remote_copy(
            src_ref=self.box.at[i],
            dst_ref=self.box.at[i],
            send_sem=self.sems.at[0, i],
            recv_sem=self.sems.at[1, i],
            device_id={"row": self.me ^ i},
            device_id_type=pl.DeviceIdType.MESH,
        )

    def gather_copy(self, i, owner):
        return pltpu.make_async_remote_copy(
            src_ref=self.full.at[self.rows(owner)],
            dst_ref=self.full.at[self.rows(owner)],
            send_sem=self.sems.at[2, i],
            recv_sem=self.sems.at[3, i],
            device_id={"row": self.me ^ i},
            device_id_type=pl.DeviceIdType.MESH,
        )

    def start(self):
        for i in range(1, self.size):
            self.own(self.me ^ i, lambda: self.scatter_copy(i).start())

    def middle(self):
        for i in range(1, self.size):
            self.own(self.me ^ i, lambda: self.scatter_copy(i).wait_send())

        def add():
            total = self.src[self.rows(self.me)]
            for i in range(1, self.size):
                self.scatter_from(i).wait_recv()
                total = total + self.box[i]
            self.full[self.rows(self.me)] = total
            self.box[0] = total

        self.own(self.me, add)

    def spread(self):
        def send():
            for i in range(1, self.size):
                self.gather_copy(i, self.me).start()

        self.own(self.me, send)

    def end(self):
        for i in range(1, self.size):
            self.own(self.me ^ i, lambda: self.gather_copy(i, self.me ^ i).wait_recv())

    def drain(self):
        def sent():
            for i in range(1, self.size):
                self.gather_copy(i, self.me).wait_send()

        self.own(self.me, sent)


def kernel(
    nrow, ncol, m_hbm, m_v, q_v, g2_v, p_v,
    a_v, s1_v, s2_v, sp_v, g1_v, c_v, box1, box2, boxp,
    in_sems, chain_sems, g_sems, sems1, sems2, semsp,
):
    me = lax.axis_index("row")
    z = lax.axis_index("col")
    height = m_v.shape[0]
    part = height // CHUNKS
    load_m = pltpu.make_async_copy(m_hbm, m_v, in_sems.at[0])
    load_a = pltpu.make_async_copy(m_hbm.at[:, pl.ds(0, B)], a_v, in_sems.at[1])

    barrier = pltpu.get_barrier_semaphore()
    for i in range(1, nrow):
        pl.semaphore_signal(
            barrier, inc=1, device_id={"row": me ^ i}, device_id_type=pl.DeviceIdType.MESH
        )
    for i in range(1, ncol):
        pl.semaphore_signal(
            barrier, inc=1, device_id={"col": z ^ i}, device_id_type=pl.DeviceIdType.MESH
        )

    pl.when(z == 0)(load_a.start)
    load_m.start()
    pl.semaphore_wait(barrier, nrow + ncol - 2)

    def chain(c):
        block = a_v.at[pl.ds(pl.multiple_of(c * part, part), part)]
        return pltpu.make_async_remote_copy(
            src_ref=block,
            dst_ref=block,
            send_sem=chain_sems.at[0, c],
            recv_sem=chain_sems.at[1, c],
            device_id={"col": lax.rem(z + 1, ncol)},
            device_id_type=pl.DeviceIdType.MESH,
        )

    passes_on = (z > 0) & (z < ncol - 1)

    def forward(c):
        chain(c).wait_recv()
        chain(c).start()

    first = Sum(nrow, me, s1_v, box1, g1_v, sems1)
    second = Sum(nrow, me, s2_v, box2, g2_v, sems2)
    coeffs = Sum(nrow, me, sp_v, boxp, p_v, semsp)

    def hand(which, total, i):
        return pltpu.make_async_remote_copy(
            src_ref=total.box.at[0],
            dst_ref=total.full.at[total.rows(me)],
            send_sem=g_sems.at[2 * which, i],
            recv_sem=g_sems.at[2 * which + 1, 0],
            device_id={"col": i},
            device_id_type=pl.DeviceIdType.MESH,
        )

    def give(which, total):
        def send():
            for i in range(1, ncol):
                hand(which, total, i).start()

        first.own(me, send)

    @pl.when(z == 0)
    def _():
        load_a.wait()
        for c in range(3):
            chain(c).start()
        s1_v[...] = mm(a_v[...], a_v[...], ((0,), (0,)))
        first.start()
        first.middle()
        give(0, first)
        first.spread()
        for c in range(3, CHUNKS):
            chain(c).start()

    @pl.when(passes_on)
    def _():
        for c in range(4):
            forward(c)

    @pl.when(z > 0)
    def _():
        first.own(me, lambda: hand(0, first, 0).wait_recv())
        first.spread()

    first.end()
    first.drain()

    def pass_on(k):
        if k % 3 == 1 and k < 12:
            pl.when(passes_on)(lambda: forward(4 + k // 3))

    factor_steps(g1_v, c_v, 0, B // S, None, pass_on)

    big = 2 * part

    @pl.when(z == 0)
    def _():
        for c in range(CHUNKS // 2):
            rows = pl.ds(c * big, big)
            q_v[rows] = mm(a_v[rows], g1_v[...], ((1,), (1,)))
        q = q_v[...]
        s2_v[...] = mm(q, q, ((0,), (0,)))
        second.start()
        load_m.wait()
        sp_v[...] = mm(q_v[...], m_v[...], ((0,), (0,)))
        second.middle()
        give(1, second)
        second.spread()
        coeffs.start()

    @pl.when(z > 0)
    def _():
        load_m.wait()
        for c in range(CHUNKS // 2):
            if c == CHUNKS // 2 - 1:
                second.own(me, lambda: hand(1, second, 0).wait_recv())
                second.spread()

            @pl.when(z == ncol - 1)
            def _():
                chain(2 * c).wait_recv()
                chain(2 * c + 1).wait_recv()

            rows = pl.ds(c * big, big)
            q = mm(a_v[rows], g1_v[...], ((1,), (1,)))
            q_v[rows] = q
            term = mm(q, m_v[rows], ((0,), (0,)))
            if c == 0:
                sp_v[...] = term
            else:
                sp_v[...] += term
        coeffs.start()

    second.end()
    second.drain()
    state = factor_steps(g2_v, c_v, 0, B // S // 2)
    coeffs.middle()
    coeffs.spread()
    factor_steps(g2_v, c_v, B // S // 2, B // S, state)
    coeffs.end()
    coeffs.drain()

    @pl.when(z == 0)
    def _():
        def given():
            for i in range(1, ncol):
                hand(0, first, i).wait_send()
                hand(1, second, i).wait_send()

        first.own(me, given)

    @pl.when(z < ncol - 1)
    def _():
        for c in range(CHUNKS):
            chain(c).wait_send()


def halves(x):
    high = x.astype(jnp.bfloat16)
    return high, (x - high.astype(jnp.float32)).astype(jnp.bfloat16)


def project_kernel(rows, m_ref, q_ref, g2_ref, p_ref, out_hbm, top_ref, out_v, back_v, sems):
    height, width = m_ref.shape
    part = height // 4
    scale = math.sqrt(rows)
    on_panel = lax.axis_index("col") == 0
    g2 = g2_ref[...]
    c = mm(g2, p_ref[...], ((1,), (0,)))
    top_ref[...] = c / scale
    back = mm(g2, c, ((0,), (0,)))
    leading = jnp.where(on_panel, -scale * g2.T, back[:, :B])
    high, low = halves(jnp.concatenate([leading, back[:, B:]], 1))
    back_v[:B] = high
    back_v[B : 2 * B] = high
    back_v[2 * B :] = low

    def store(i):
        block = pl.ds(i * part, part)
        return pltpu.make_async_copy(out_v.at[block], out_hbm.at[block], sems.at[i])

    for i in range(4):
        block = pl.ds(i * part, part)
        high, low = halves(q_ref[block])
        change = jnp.dot(
            jnp.concatenate([high, low, high], 1), back_v[...], preferred_element_type=jnp.float32
        )
        base = m_ref[block]
        out_v[block, :B] = jnp.where(on_panel, 0.0, base[:, :B]) - change[:, :B]
        out_v[block, B:] = base[:, B:] - change[:, B:]
        store(i).start()
    for i in range(4):
        store(i).wait()


def on_device(nrow, ncol, matrix):
    height, width = matrix.shape
    slab = max(8, B // nrow)
    f32 = jnp.float32
    dma = pltpu.SemaphoreType.DMA
    shape = jax.ShapeDtypeStruct
    held, basis, inverse, coeffs = pl.pallas_call(
        functools.partial(kernel, nrow, ncol),
        out_shape=(
            shape((height, width), f32), shape((height, B), f32), shape((B, B), f32), shape((B, width), f32)
        ),
        in_specs=[pl.BlockSpec(memory_space=pltpu.HBM)],
        out_specs=(pl.BlockSpec(memory_space=pltpu.VMEM),) * 4,
        scratch_shapes=[
            pltpu.VMEM((height, B), f32),
            pltpu.VMEM((B, B), f32),
            pltpu.VMEM((B, B), f32),
            pltpu.VMEM((B, width), f32),
            pltpu.VMEM((B, B), f32),
            pltpu.VMEM((S * S, B), f32),
            pltpu.VMEM((nrow, slab, B), f32),
            pltpu.VMEM((nrow, slab, B), f32),
            pltpu.VMEM((nrow, slab, width), f32),
            dma((2,)),
            dma((2, CHUNKS)),
            dma((4, ncol)),
            dma((4, nrow)),
            dma((4, nrow)),
            dma((4, nrow)),
        ],
        compiler_params=pltpu.CompilerParams(
            collective_id=0, has_side_effects=True, vmem_limit_bytes=12 * 2**20
        ),
    )(pltpu.with_memory_space_constraint(matrix, pltpu.HBM))
    whole = pl.BlockSpec(memory_space=pltpu.VMEM)
    return pl.pallas_call(
        functools.partial(project_kernel, height * nrow),
        out_shape=(shape((height, width), f32), shape((B, width), f32)),
        in_specs=[whole] * 4,
        out_specs=(pl.BlockSpec(memory_space=pl.ANY), whole),
        scratch_shapes=[
            pltpu.VMEM((height, width), f32),
            pltpu.VMEM((3 * B, width), jnp.bfloat16),
            dma((4,)),
        ],
        compiler_params=pltpu.CompilerParams(vmem_limit_bytes=12 * 2**20),
    )(held, basis, inverse, coeffs)


def solution(mesh):
    nrow, ncol = mesh.shape["row"], mesh.shape["col"]
    return jax.shard_map(
        functools.partial(on_device, nrow, ncol),
        mesh=mesh,
        in_specs=(P("row", "col"),),
        out_specs=(P("row", "col"), P(None, "col")),
        check_vma=False,
    )
```

```python
import functools
import math

import jax
import jax.numpy as jnp
from jax import lax
from jax.experimental import pallas as pl
from jax.experimental.pallas import tpu as pltpu
from jax.sharding import PartitionSpec as P

B = 128
S = 8
CHUNKS = 8
EARLY = 3
NEAR = {-1: (3, 4, 5, 6, 7)}
LAST = 3
COLLECT = {7: (0, 1, 2, 3)}
FAR = {-1: (3, 4), 1: (5,), 5: (6,), 9: (7,)}
HI = lax.Precision.HIGHEST


def mm(left, right, dims):
    return lax.dot_general(
        left, right, (dims, ((), ())), precision=HI, preferred_element_type=jnp.float32
    )


def thirds(x):
    high = x.astype(jnp.bfloat16).astype(jnp.float32)
    rest = x - high
    mid = rest.astype(jnp.bfloat16).astype(jnp.float32)
    return high, mid, rest - mid


def self_product(t):
    high, mid, low = thirds(t)
    left = jnp.concatenate([high, high, mid, mid, high, low], 0).astype(jnp.bfloat16)
    right = jnp.concatenate([high, mid, high, mid, low, high], 0).astype(jnp.bfloat16)
    return lax.dot_general(
        left, right, (((0,), (0,)), ((), ())), preferred_element_type=jnp.float32
    )


def factor_steps(w_ref, c_ref, low, high, state=None, after_step=None):
    lane = lax.broadcasted_iota(jnp.int32, (S, B), 1)
    sub = lax.broadcasted_iota(jnp.int32, (S, B), 0)
    count = B // S
    w = [w_ref[S * r : S * r + S] for r in range(count)] if state is None else state
    for k in range(low, high):
        here = (lane >= S * k) & (lane < S * k + S)
        rows = w[k]
        d = {}
        for j in range(S):
            c_ref[S * j : S * j + S] = jnp.broadcast_to(
                rows[:, S * k + j : S * k + j + 1], (S, B)
            )
            for i in range(j, S):
                d[i, j] = jnp.broadcast_to(c_ref[S * j + i : S * j + i + 1], (S, B))
        rows = jnp.where(here, jnp.where(lane - S * k == sub, 1.0, 0.0), rows)
        p = [jnp.broadcast_to(rows[j : j + 1], (S, B)) for j in range(S)]
        t = None
        for j in range(S):
            inv = lax.rsqrt(d[j, j])
            l = {i: d[i, j] * inv for i in range(j + 1, S)}
            for i in range(j + 1, S):
                for m in range(j + 1, i + 1):
                    d[i, m] = d[i, m] - l[i] * l[m]
            tj = p[j] * inv
            for i in range(j + 1, S):
                p[i] = p[i] - l[i] * tj
            t = tj if t is None else jnp.where(sub == j, tj, t)
        w_ref[S * k : S * k + S] = jnp.where(lane < S * k + S, t, 0.0)
        if k + 1 < count:
            after = jnp.where(here, 0.0, w[k + 1])
            for i in range(S):
                at = S * (k + 1) + i
                column = jnp.broadcast_to(t[:, at : at + 1], (S, B))
                drop = jnp.sum(column * t, axis=0, keepdims=True)
                after = jnp.where(sub == i, after - drop, after)
            w[k + 1] = after
        if k + 2 < count:
            change = self_product(t)
            for r in range(k + 2, count):
                w[r] = jnp.where(here, 0.0, w[r]) - change[S * r : S * r + S]
        if after_step is not None:
            after_step(k)
    return w


class Sum:
    def __init__(self, size, me, src, box, full, sems):
        self.size, self.me, self.src, self.box, self.full = size, me, src, box, full
        self.sems = sems
        self.slab = max(8, B // size)
        self.owners = B // self.slab

    def rows(self, owner):
        return pl.ds(pl.multiple_of(owner * self.slab, self.slab), self.slab)

    def own(self, device, what):
        if self.owners == self.size:
            what()
        else:
            pl.when(device < self.owners)(what)

    def scatter_copy(self, i):
        peer = self.me ^ i
        return pltpu.make_async_remote_copy(
            src_ref=self.src.at[self.rows(peer)],
            dst_ref=self.box.at[i],
            send_sem=self.sems.at[0, i],
            recv_sem=self.sems.at[1, i],
            device_id={"row": peer},
            device_id_type=pl.DeviceIdType.MESH,
        )

    def scatter_from(self, i):
        return pltpu.make_async_remote_copy(
            src_ref=self.box.at[i],
            dst_ref=self.box.at[i],
            send_sem=self.sems.at[0, i],
            recv_sem=self.sems.at[1, i],
            device_id={"row": self.me ^ i},
            device_id_type=pl.DeviceIdType.MESH,
        )

    def gather_copy(self, i, owner):
        return pltpu.make_async_remote_copy(
            src_ref=self.full.at[self.rows(owner)],
            dst_ref=self.full.at[self.rows(owner)],
            send_sem=self.sems.at[2, i],
            recv_sem=self.sems.at[3, i],
            device_id={"row": self.me ^ i},
            device_id_type=pl.DeviceIdType.MESH,
        )

    def start(self):
        for i in range(1, self.size):
            self.own(self.me ^ i, lambda: self.scatter_copy(i).start())

    def middle(self):
        for i in range(1, self.size):
            self.own(self.me ^ i, lambda: self.scatter_copy(i).wait_send())

        def add():
            total = self.src[self.rows(self.me)]
            for i in range(1, self.size):
                self.scatter_from(i).wait_recv()
                total = total + self.box[i]
            self.full[self.rows(self.me)] = total
            self.box[0] = total

        self.own(self.me, add)

    def spread(self):
        def send():
            for i in range(1, self.size):
                self.gather_copy(i, self.me).start()

        self.own(self.me, send)

    def end(self):
        for i in range(1, self.size):
            self.own(self.me ^ i, lambda: self.gather_copy(i, self.me ^ i).wait_recv())

    def drain(self):
        def sent():
            for i in range(1, self.size):
                self.gather_copy(i, self.me).wait_send()

        self.own(self.me, sent)


class PairSum:
    def __init__(self, size, me, src, pair, gather, full, pair_sems, chip_sems):
        self.chips, self.me, self.core, self.chip = size // 2, me, me % 2, me // 2
        self.src, self.pair, self.gather, self.full = src, pair, gather, full
        self.pair_sems, self.chip_sems = pair_sems, chip_sems
        self.half = B // 2
        self.parts = src.shape[1] // B

    def rows(self, core):
        return pl.ds(pl.multiple_of(core * self.half, self.half), self.half)

    def swap_copy(self, c):
        cols = pl.ds(c * B, B)
        return pltpu.make_async_remote_copy(
            src_ref=self.src.at[self.rows(1 - self.core), cols],
            dst_ref=self.pair.at[:, cols],
            send_sem=self.pair_sems.at[0, c],
            recv_sem=self.pair_sems.at[1, c],
            device_id={"row": self.me ^ 1},
            device_id_type=pl.DeviceIdType.MESH,
        )

    def chip_copy(self, c, i, slot):
        cols = pl.ds(c * B, B)
        return pltpu.make_async_remote_copy(
            src_ref=self.gather.at[slot, :, cols],
            dst_ref=self.gather.at[slot, :, cols],
            send_sem=self.chip_sems.at[0, c, i],
            recv_sem=self.chip_sems.at[1, c, i],
            device_id={"row": self.me ^ (2 * i)},
            device_id_type=pl.DeviceIdType.MESH,
        )

    def back_copy(self, c, core):
        cols = pl.ds(c * B, B)
        return pltpu.make_async_remote_copy(
            src_ref=self.full.at[self.rows(core), cols],
            dst_ref=self.full.at[self.rows(core), cols],
            send_sem=self.pair_sems.at[2, c],
            recv_sem=self.pair_sems.at[3, c],
            device_id={"row": self.me ^ 1},
            device_id_type=pl.DeviceIdType.MESH,
        )

    def swap(self):
        for c in range(self.parts):
            self.swap_copy(c).start()

    def spread(self):
        for c in range(self.parts):
            cols = pl.ds(c * B, B)
            self.swap_copy(c).wait_recv()
            self.gather[self.chip, :, cols] = self.src[self.rows(self.core), cols] + self.pair[:, cols]
            for i in range(self.chips - 1, 0, -1):
                self.chip_copy(c, i, self.chip).start()

    def collect(self, c):
        cols = pl.ds(c * B, B)
        for i in range(1, self.chips):
            self.chip_copy(c, i, self.chip ^ i).wait_recv()
        total = self.gather[0, :, cols]
        for i in range(1, self.chips):
            total = total + self.gather[i, :, cols]
        self.full[self.rows(self.core), cols] = total
        self.back_copy(c, self.core).start()

    def end(self):
        for c in range(self.parts):
            self.back_copy(c, 1 - self.core).wait_recv()

    def drain(self):
        for c in range(self.parts):
            self.swap_copy(c).wait_send()
            self.back_copy(c, self.core).wait_send()
            for i in range(1, self.chips):
                self.chip_copy(c, i, self.chip).wait_send()


def kernel(
    nrow, ncol, m_hbm, m_v, q_v, g2_v, p_v,
    a_v, s1_v, s2_v, sp_v, g1_v, c_v, box1, box2, pair_v, gather_v,
    in_sems, chain_sems, g_sems, sems1, sems2, pair_sems, chip_sems, ready,
):
    me = lax.axis_index("row")
    z = lax.axis_index("col")
    height = m_v.shape[0]
    part = height // CHUNKS
    load_m = pltpu.make_async_copy(m_hbm, m_v, in_sems.at[0])
    load_a = pltpu.make_async_copy(m_hbm.at[:, pl.ds(0, B)], a_v, in_sems.at[1])

    barrier = pltpu.get_barrier_semaphore()
    for i in range(1, nrow):
        pl.semaphore_signal(
            barrier, inc=1, device_id={"row": me ^ i}, device_id_type=pl.DeviceIdType.MESH
        )

    def greet(sem, column):
        pl.semaphore_signal(
            sem, inc=1, device_id={"col": column}, device_id_type=pl.DeviceIdType.MESH
        )

    @pl.when(z > 0)
    def _():
        greet(barrier, z - 1)

    @pl.when(z == 0)
    def _():
        load_a.start()
        for i in range(2, ncol):
            greet(barrier, i)

    load_m.start()

    def enter():
        sends_on = jnp.where(z < ncol - 1, 1, 0)
        far = jnp.where(z > 1, 1, 0)
        pl.semaphore_wait(barrier, nrow - 1 + sends_on + far)

    first = Sum(nrow, me, s1_v, box1, g1_v, sems1)
    second = Sum(nrow, me, s2_v, box2, g2_v, sems2)
    coeffs = PairSum(nrow, me, sp_v, pair_v, gather_v, p_v, pair_sems, chip_sems)

    @pl.when(z == 0)
    def _():
        load_a.wait()
        s1_v[...] = mm(a_v[...], a_v[...], ((0,), (0,)))

    enter()

    @pl.when(z > 1)
    def _():
        greet(ready, 0)

    def chain(c):
        block = a_v.at[pl.ds(pl.multiple_of(c * part, part), part)]
        return pltpu.make_async_remote_copy(
            src_ref=block,
            dst_ref=block,
            send_sem=chain_sems.at[0, c],
            recv_sem=chain_sems.at[1, c],
            device_id={"col": lax.rem(z + 1, ncol)},
            device_id_type=pl.DeviceIdType.MESH,
        )

    passes_on = (z > 0) & (z < ncol - 1)

    def forward(*chunks):
        for c in chunks:
            chain(c).wait_recv()
            chain(c).start()

    def hand(which, total, i):
        return pltpu.make_async_remote_copy(
            src_ref=total.box.at[0],
            dst_ref=total.full.at[total.rows(me)],
            send_sem=g_sems.at[2 * which, i],
            recv_sem=g_sems.at[2 * which + 1, 0],
            device_id={"col": i},
            device_id_type=pl.DeviceIdType.MESH,
        )

    def give(which, total):
        def send():
            for i in range(ncol - 1, 0, -1):
                hand(which, total, i).start()

        first.own(me, send)

    @pl.when(z == 0)
    def _():
        for c in range(EARLY):
            chain(c).start()
        first.start()
        first.middle()
        if ncol > 2:
            pl.semaphore_wait(ready, ncol - 2)
        give(0, first)
        first.spread()
        for c in range(EARLY, CHUNKS):
            chain(c).start()

    @pl.when(passes_on)
    def _():
        forward(*range(EARLY))

    @pl.when(z > 0)
    def _():
        first.own(me, lambda: hand(0, first, 0).wait_recv())
        first.spread()

    def pass_on(k):
        near, far = NEAR.get(k, ()), FAR.get(k, ())
        if near:
            pl.when(passes_on & (z == 1))(lambda: forward(*near))
        if far:
            pl.when(passes_on & (z > 1))(lambda: forward(*far))

    pass_on(-1)
    first.end()
    first.drain()
    factor_steps(g1_v, c_v, 0, B // S, None, pass_on)

    big = 2 * part

    @pl.when(z == 0)
    def _():
        for c in range(CHUNKS // 2):
            rows = pl.ds(c * big, big)
            q_v[rows] = mm(a_v[rows], g1_v[...], ((1,), (1,)))
        q = q_v[...]
        s2_v[...] = mm(q, q, ((0,), (0,)))
        second.start()
        load_m.wait()
        sp_v[...] = mm(q_v[...], m_v[...], ((0,), (0,)))
        coeffs.swap()
        second.middle()
        give(1, second)
        second.spread()
        coeffs.spread()

    @pl.when(z > 0)
    def _():
        load_m.wait()
        def share():
            second.own(me, lambda: hand(1, second, 0).wait_recv())
            second.spread()

        for c in range(CHUNKS // 2):
            if c == LAST:
                share()

            @pl.when(z == ncol - 1)
            def _():
                chain(2 * c).wait_recv()
                chain(2 * c + 1).wait_recv()

            rows = pl.ds(c * big, big)
            q = mm(a_v[rows], g1_v[...], ((1,), (1,)))
            q_v[rows] = q
            term = mm(q, m_v[rows], ((0,), (0,)))
            if c == 0:
                sp_v[...] = term
            else:
                sp_v[...] += term
        coeffs.swap()
        coeffs.spread()

    second.end()
    second.drain()

    def collect(k):
        for c in COLLECT.get(k, ()):
            if c < coeffs.parts:
                coeffs.collect(c)

    factor_steps(g2_v, c_v, 0, B // S, None, collect)
    for c in range(max(sum(COLLECT.values(), ())) + 1, coeffs.parts):
        coeffs.collect(c)
    coeffs.end()
    coeffs.drain()

    @pl.when(z == 0)
    def _():
        def given():
            for i in range(1, ncol):
                hand(0, first, i).wait_send()
                hand(1, second, i).wait_send()

        first.own(me, given)

    @pl.when(z < ncol - 1)
    def _():
        for c in range(CHUNKS):
            chain(c).wait_send()


def halves(x):
    high = x.astype(jnp.bfloat16)
    return high, (x - high.astype(jnp.float32)).astype(jnp.bfloat16)


def project_kernel(rows, m_ref, q_ref, g2_ref, p_ref, out_hbm, top_ref, out_v, back_v, sems):
    height, width = m_ref.shape
    part = height // 4
    scale = math.sqrt(rows)
    on_panel = lax.axis_index("col") == 0
    g2 = g2_ref[...]
    c = mm(g2, p_ref[...], ((1,), (0,)))
    top_ref[...] = c / scale
    back = mm(g2, c, ((0,), (0,)))
    leading = jnp.where(on_panel, -scale * g2.T, back[:, :B])
    high, low = halves(jnp.concatenate([leading, back[:, B:]], 1))
    back_v[:B] = high
    back_v[B : 2 * B] = high
    back_v[2 * B :] = low

    def store(i):
        block = pl.ds(i * part, part)
        return pltpu.make_async_copy(out_v.at[block], out_hbm.at[block], sems.at[i])

    for i in range(4):
        block = pl.ds(i * part, part)
        high, low = halves(q_ref[block])
        change = jnp.dot(
            jnp.concatenate([high, low, high], 1), back_v[...], preferred_element_type=jnp.float32
        )
        base = m_ref[block]
        out_v[block, :B] = jnp.where(on_panel, 0.0, base[:, :B]) - change[:, :B]
        out_v[block, B:] = base[:, B:] - change[:, B:]
        store(i).start()
    for i in range(4):
        store(i).wait()


def on_device(nrow, ncol, matrix):
    height, width = matrix.shape
    slab = max(8, B // nrow)
    f32 = jnp.float32
    dma = pltpu.SemaphoreType.DMA
    shape = jax.ShapeDtypeStruct
    held, basis, inverse, coeffs = pl.pallas_call(
        functools.partial(kernel, nrow, ncol),
        out_shape=(
            shape((height, width), f32), shape((height, B), f32), shape((B, B), f32), shape((B, width), f32)
        ),
        in_specs=[pl.BlockSpec(memory_space=pltpu.HBM)],
        out_specs=(pl.BlockSpec(memory_space=pltpu.VMEM),) * 4,
        scratch_shapes=[
            pltpu.VMEM((height, B), f32),
            pltpu.VMEM((B, B), f32),
            pltpu.VMEM((B, B), f32),
            pltpu.VMEM((B, width), f32),
            pltpu.VMEM((B, B), f32),
            pltpu.VMEM((S * S, B), f32),
            pltpu.VMEM((nrow, slab, B), f32),
            pltpu.VMEM((nrow, slab, B), f32),
            pltpu.VMEM((B // 2, width), f32),
            pltpu.VMEM((nrow // 2, B // 2, width), f32),
            dma((2,)),
            dma((2, CHUNKS)),
            dma((4, ncol)),
            dma((4, nrow)),
            dma((4, nrow)),
            dma((4, width // B)),
            dma((2, width // B, nrow // 2)),
            pltpu.SemaphoreType.REGULAR,
        ],
        compiler_params=pltpu.CompilerParams(
            collective_id=0, has_side_effects=True, vmem_limit_bytes=12 * 2**20
        ),
    )(pltpu.with_memory_space_constraint(matrix, pltpu.HBM))
    whole = pl.BlockSpec(memory_space=pltpu.VMEM)
    return pl.pallas_call(
        functools.partial(project_kernel, height * nrow),
        out_shape=(shape((height, width), f32), shape((B, width), f32)),
        in_specs=[whole] * 4,
        out_specs=(pl.BlockSpec(memory_space=pl.ANY), whole),
        scratch_shapes=[
            pltpu.VMEM((height, width), f32),
            pltpu.VMEM((3 * B, width), jnp.bfloat16),
            dma((4,)),
        ],
        compiler_params=pltpu.CompilerParams(vmem_limit_bytes=12 * 2**20),
    )(held, basis, inverse, coeffs)


def solution(mesh):
    nrow, ncol = mesh.shape["row"], mesh.shape["col"]
    return jax.shard_map(
        functools.partial(on_device, nrow, ncol),
        mesh=mesh,
        in_specs=(P("row", "col"),),
        out_specs=(P("row", "col"), P(None, "col")),
        check_vma=False,
    )
```

```python
import functools
import math

import jax
import jax.numpy as jnp
from jax import lax
from jax.experimental import pallas as pl
from jax.experimental.pallas import tpu as pltpu
from jax.sharding import PartitionSpec as P

B = 128
S = 8
CHUNKS = 8
EARLY = 3
NEAR = {-1: (3, 4, 5, 6, 7)}
LAST = 3
COLLECT = {7: (0, 1, 2, 3)}
FAR = {-1: (3, 4), 1: (5,), 5: (6,), 9: (7,)}
HI = lax.Precision.HIGHEST


def mm(left, right, dims):
    return lax.dot_general(
        left, right, (dims, ((), ())), precision=HI, preferred_element_type=jnp.float32
    )


def thirds(x):
    high = x.astype(jnp.bfloat16).astype(jnp.float32)
    rest = x - high
    mid = rest.astype(jnp.bfloat16).astype(jnp.float32)
    return high, mid, rest - mid


def self_product(t):
    high, mid, low = thirds(t)
    left = jnp.concatenate([high, high, mid, mid, high, low], 0).astype(jnp.bfloat16)
    right = jnp.concatenate([high, mid, high, mid, low, high], 0).astype(jnp.bfloat16)
    return lax.dot_general(
        left, right, (((0,), (0,)), ((), ())), preferred_element_type=jnp.float32
    )


def spread_block(c_ref, rows, k):
    for j in range(S):
        c_ref[S * j : S * j + S] = jnp.broadcast_to(
            rows[:, S * k + j : S * k + j + 1], (S, B)
        )
    return {
        (i, j): jnp.broadcast_to(c_ref[S * j + i : S * j + i + 1], (S, B))
        for j in range(S)
        for i in range(j, S)
    }


def factor_steps(w_ref, c_ref, after_step):
    lane = lax.broadcasted_iota(jnp.int32, (S, B), 1)
    sub = lax.broadcasted_iota(jnp.int32, (S, B), 0)
    count = B // S
    w = [w_ref[S * r : S * r + S] for r in range(count)]
    d = spread_block(c_ref, w[0], 0)
    for k in range(count):
        here = (lane >= S * k) & (lane < S * k + S)
        following = spread_block(c_ref, w[k + 1], k + 1) if k + 1 < count else None
        rows = jnp.where(here, jnp.where(lane - S * k == sub, 1.0, 0.0), w[k])
        p = [jnp.broadcast_to(rows[j : j + 1], (S, B)) for j in range(S)]
        t = None
        for j in range(S):
            inv = lax.rsqrt(d[j, j])
            l = {i: d[i, j] * inv for i in range(j + 1, S)}
            for i in range(j + 1, S):
                for m in range(j + 1, i + 1):
                    d[i, m] = d[i, m] - l[i] * l[m]
            tj = p[j] * inv
            for i in range(j + 1, S):
                p[i] = p[i] - l[i] * tj
            t = tj if t is None else jnp.where(sub == j, tj, t)
        w_ref[S * k : S * k + S] = jnp.where(lane < S * k + S, t, 0.0)
        if k + 1 < count:
            at = S * (k + 1)
            columns = [jnp.broadcast_to(t[:, at + i : at + i + 1], (S, B)) for i in range(S)]

            def drop(i, what):
                return jnp.sum(columns[i] * what, axis=0, keepdims=True)

            d = {
                (i, j): following[i, j] - jnp.broadcast_to(drop(i, columns[j]), (S, B))
                for (i, j) in following
            }
            after = jnp.where(here, 0.0, w[k + 1])
            for i in range(S):
                after = jnp.where(sub == i, after - drop(i, t), after)
            w[k + 1] = after
        if k + 2 < count:
            change = self_product(t)
            for r in range(k + 2, count):
                w[r] = jnp.where(here, 0.0, w[r]) - change[S * r : S * r + S]
        after_step(k)


class Sum:
    def __init__(self, size, me, src, box, full, sems):
        self.size, self.me, self.src, self.box, self.full = size, me, src, box, full
        self.sems = sems
        self.slab = max(8, B // size)
        self.owners = B // self.slab

    def rows(self, owner):
        return pl.ds(pl.multiple_of(owner * self.slab, self.slab), self.slab)

    def own(self, device, what):
        if self.owners == self.size:
            what()
        else:
            pl.when(device < self.owners)(what)

    def scatter_copy(self, i):
        peer = self.me ^ i
        return pltpu.make_async_remote_copy(
            src_ref=self.src.at[self.rows(peer)],
            dst_ref=self.box.at[i],
            send_sem=self.sems.at[0, i],
            recv_sem=self.sems.at[1, i],
            device_id={"row": peer},
            device_id_type=pl.DeviceIdType.MESH,
        )

    def scatter_from(self, i):
        return pltpu.make_async_remote_copy(
            src_ref=self.box.at[i],
            dst_ref=self.box.at[i],
            send_sem=self.sems.at[0, i],
            recv_sem=self.sems.at[1, i],
            device_id={"row": self.me ^ i},
            device_id_type=pl.DeviceIdType.MESH,
        )

    def gather_copy(self, i, owner):
        return pltpu.make_async_remote_copy(
            src_ref=self.full.at[self.rows(owner)],
            dst_ref=self.full.at[self.rows(owner)],
            send_sem=self.sems.at[2, i],
            recv_sem=self.sems.at[3, i],
            device_id={"row": self.me ^ i},
            device_id_type=pl.DeviceIdType.MESH,
        )

    def start(self):
        for i in range(1, self.size):
            self.own(self.me ^ i, lambda: self.scatter_copy(i).start())

    def middle(self):
        for i in range(1, self.size):
            self.own(self.me ^ i, lambda: self.scatter_copy(i).wait_send())

        def add():
            total = self.src[self.rows(self.me)]
            for i in range(1, self.size):
                self.scatter_from(i).wait_recv()
                total = total + self.box[i]
            self.full[self.rows(self.me)] = total
            self.box[0] = total

        self.own(self.me, add)

    def spread(self):
        def send():
            for i in range(1, self.size):
                self.gather_copy(i, self.me).start()

        self.own(self.me, send)

    def end(self):
        for i in range(1, self.size):
            self.own(self.me ^ i, lambda: self.gather_copy(i, self.me ^ i).wait_recv())

    def drain(self):
        def sent():
            for i in range(1, self.size):
                self.gather_copy(i, self.me).wait_send()

        self.own(self.me, sent)


class PairSum:
    def __init__(self, size, me, src, pair, gather, full, pair_sems, chip_sems):
        self.chips, self.me, self.core, self.chip = size // 2, me, me % 2, me // 2
        self.src, self.pair, self.gather, self.full = src, pair, gather, full
        self.pair_sems, self.chip_sems = pair_sems, chip_sems
        self.half = B // 2
        self.parts = src.shape[1] // B

    def rows(self, core):
        return pl.ds(pl.multiple_of(core * self.half, self.half), self.half)

    def swap_copy(self, c):
        cols = pl.ds(c * B, B)
        return pltpu.make_async_remote_copy(
            src_ref=self.src.at[self.rows(1 - self.core), cols],
            dst_ref=self.pair.at[:, cols],
            send_sem=self.pair_sems.at[0, c],
            recv_sem=self.pair_sems.at[1, c],
            device_id={"row": self.me ^ 1},
            device_id_type=pl.DeviceIdType.MESH,
        )

    def chip_copy(self, c, i, slot):
        cols = pl.ds(c * B, B)
        return pltpu.make_async_remote_copy(
            src_ref=self.gather.at[slot, :, cols],
            dst_ref=self.gather.at[slot, :, cols],
            send_sem=self.chip_sems.at[0, c, i],
            recv_sem=self.chip_sems.at[1, c, i],
            device_id={"row": self.me ^ (2 * i)},
            device_id_type=pl.DeviceIdType.MESH,
        )

    def back_copy(self, c, core):
        cols = pl.ds(c * B, B)
        return pltpu.make_async_remote_copy(
            src_ref=self.full.at[self.rows(core), cols],
            dst_ref=self.full.at[self.rows(core), cols],
            send_sem=self.pair_sems.at[2, c],
            recv_sem=self.pair_sems.at[3, c],
            device_id={"row": self.me ^ 1},
            device_id_type=pl.DeviceIdType.MESH,
        )

    def swap(self):
        for c in range(self.parts):
            self.swap_copy(c).start()

    def spread(self):
        for c in range(self.parts):
            cols = pl.ds(c * B, B)
            self.swap_copy(c).wait_recv()
            self.gather[self.chip, :, cols] = self.src[self.rows(self.core), cols] + self.pair[:, cols]
            for i in range(self.chips - 1, 0, -1):
                self.chip_copy(c, i, self.chip).start()

    def collect(self, c):
        cols = pl.ds(c * B, B)
        for i in range(1, self.chips):
            self.chip_copy(c, i, self.chip ^ i).wait_recv()
        total = self.gather[0, :, cols]
        for i in range(1, self.chips):
            total = total + self.gather[i, :, cols]
        self.full[self.rows(self.core), cols] = total
        self.back_copy(c, self.core).start()

    def end(self):
        for c in range(self.parts):
            self.back_copy(c, 1 - self.core).wait_recv()

    def drain(self):
        for c in range(self.parts):
            self.swap_copy(c).wait_send()
            self.back_copy(c, self.core).wait_send()
            for i in range(1, self.chips):
                self.chip_copy(c, i, self.chip).wait_send()


def kernel(
    nrow, ncol, m_hbm, m_v, q_v, g2_v, p_v,
    a_v, s1_v, s2_v, sp_v, g1_v, c_v, box1, box2, pair_v, gather_v,
    in_sems, chain_sems, g_sems, sems1, sems2, pair_sems, chip_sems, ready,
):
    me = lax.axis_index("row")
    z = lax.axis_index("col")
    height = m_v.shape[0]
    part = height // CHUNKS
    load_m = pltpu.make_async_copy(m_hbm, m_v, in_sems.at[0])
    load_a = pltpu.make_async_copy(m_hbm.at[:, pl.ds(0, B)], a_v, in_sems.at[1])

    barrier = pltpu.get_barrier_semaphore()
    for i in range(1, nrow):
        pl.semaphore_signal(
            barrier, inc=1, device_id={"row": me ^ i}, device_id_type=pl.DeviceIdType.MESH
        )

    def greet(sem, column):
        pl.semaphore_signal(
            sem, inc=1, device_id={"col": column}, device_id_type=pl.DeviceIdType.MESH
        )

    @pl.when(z > 0)
    def _():
        greet(barrier, z - 1)

    @pl.when(z == 0)
    def _():
        load_a.start()
        for i in range(2, ncol):
            greet(barrier, i)

    load_m.start()

    def enter():
        sends_on = jnp.where(z < ncol - 1, 1, 0)
        far = jnp.where(z > 1, 1, 0)
        pl.semaphore_wait(barrier, nrow - 1 + sends_on + far)

    first = Sum(nrow, me, s1_v, box1, g1_v, sems1)
    second = Sum(nrow, me, s2_v, box2, g2_v, sems2)
    coeffs = PairSum(nrow, me, sp_v, pair_v, gather_v, p_v, pair_sems, chip_sems)

    @pl.when(z == 0)
    def _():
        load_a.wait()
        s1_v[...] = mm(a_v[...], a_v[...], ((0,), (0,)))

    enter()

    @pl.when(z > 1)
    def _():
        greet(ready, 0)

    def chain(c):
        block = a_v.at[pl.ds(pl.multiple_of(c * part, part), part)]
        return pltpu.make_async_remote_copy(
            src_ref=block,
            dst_ref=block,
            send_sem=chain_sems.at[0, c],
            recv_sem=chain_sems.at[1, c],
            device_id={"col": lax.rem(z + 1, ncol)},
            device_id_type=pl.DeviceIdType.MESH,
        )

    passes_on = (z > 0) & (z < ncol - 1)

    def forward(*chunks):
        for c in chunks:
            chain(c).wait_recv()
            chain(c).start()

    def hand(which, total, i):
        return pltpu.make_async_remote_copy(
            src_ref=total.box.at[0],
            dst_ref=total.full.at[total.rows(me)],
            send_sem=g_sems.at[2 * which, i],
            recv_sem=g_sems.at[2 * which + 1, 0],
            device_id={"col": i},
            device_id_type=pl.DeviceIdType.MESH,
        )

    def give(which, total):
        def send():
            for i in range(ncol - 1, 0, -1):
                hand(which, total, i).start()

        first.own(me, send)

    @pl.when(z == 0)
    def _():
        for c in range(EARLY):
            chain(c).start()
        first.start()
        first.middle()
        if ncol > 2:
            pl.semaphore_wait(ready, ncol - 2)
        give(0, first)
        first.spread()
        for c in range(EARLY, CHUNKS):
            chain(c).start()

    @pl.when(passes_on)
    def _():
        forward(*range(EARLY))

    @pl.when(z > 0)
    def _():
        first.own(me, lambda: hand(0, first, 0).wait_recv())
        first.spread()

    def pass_on(k):
        near, far = NEAR.get(k, ()), FAR.get(k, ())
        if near:
            pl.when(passes_on & (z == 1))(lambda: forward(*near))
        if far:
            pl.when(passes_on & (z > 1))(lambda: forward(*far))

    pass_on(-1)
    first.end()
    first.drain()
    factor_steps(g1_v, c_v, pass_on)

    big = 2 * part

    @pl.when(z == 0)
    def _():
        for c in range(CHUNKS // 2):
            rows = pl.ds(c * big, big)
            q_v[rows] = mm(a_v[rows], g1_v[...], ((1,), (1,)))
        q = q_v[...]
        s2_v[...] = mm(q, q, ((0,), (0,)))
        second.start()
        load_m.wait()
        sp_v[...] = mm(q_v[...], m_v[...], ((0,), (0,)))
        coeffs.swap()
        second.middle()
        give(1, second)
        second.spread()
        coeffs.spread()

    @pl.when(z > 0)
    def _():
        load_m.wait()
        def share():
            second.own(me, lambda: hand(1, second, 0).wait_recv())
            second.spread()

        for c in range(CHUNKS // 2):
            if c == LAST:
                share()

            @pl.when(z == ncol - 1)
            def _():
                chain(2 * c).wait_recv()
                chain(2 * c + 1).wait_recv()

            rows = pl.ds(c * big, big)
            q = mm(a_v[rows], g1_v[...], ((1,), (1,)))
            q_v[rows] = q
            term = mm(q, m_v[rows], ((0,), (0,)))
            if c == 0:
                sp_v[...] = term
            else:
                sp_v[...] += term
        coeffs.swap()
        coeffs.spread()

    second.end()
    second.drain()

    def collect(k):
        for c in COLLECT.get(k, ()):
            if c < coeffs.parts:
                coeffs.collect(c)

    factor_steps(g2_v, c_v, collect)
    for c in range(max(sum(COLLECT.values(), ())) + 1, coeffs.parts):
        coeffs.collect(c)
    coeffs.end()
    coeffs.drain()

    @pl.when(z == 0)
    def _():
        def given():
            for i in range(1, ncol):
                hand(0, first, i).wait_send()
                hand(1, second, i).wait_send()

        first.own(me, given)

    @pl.when(z < ncol - 1)
    def _():
        for c in range(CHUNKS):
            chain(c).wait_send()


def halves(x):
    high = x.astype(jnp.bfloat16)
    return high, (x - high.astype(jnp.float32)).astype(jnp.bfloat16)


def project_kernel(rows, m_ref, q_ref, g2_ref, p_ref, out_hbm, top_hbm, out_v, top_v, back_v, sems):
    height, width = m_ref.shape
    part = height // 4
    scale = math.sqrt(rows)
    on_panel = lax.axis_index("col") == 0
    g2 = g2_ref[...]
    c = mm(g2, p_ref[...], ((1,), (0,)))
    back = mm(g2, c, ((0,), (0,)))
    leading = jnp.where(on_panel, -scale * g2.T, back[:, :B])
    high, low = halves(jnp.concatenate([leading, back[:, B:]], 1))
    back_v[:B] = high
    back_v[B : 2 * B] = high
    back_v[2 * B :] = low

    top_v[...] = c / scale
    top_store = pltpu.make_async_copy(top_v, top_hbm, sems.at[4])
    top_store.start()

    def store(i):
        block = pl.ds(i * part, part)
        return pltpu.make_async_copy(out_v.at[block], out_hbm.at[block], sems.at[i])

    for i in range(4):
        block = pl.ds(i * part, part)
        high, low = halves(q_ref[block])
        change = jnp.dot(
            jnp.concatenate([high, low, high], 1), back_v[...], preferred_element_type=jnp.float32
        )
        base = m_ref[block]
        out_v[block, :B] = jnp.where(on_panel, 0.0, base[:, :B]) - change[:, :B]
        out_v[block, B:] = base[:, B:] - change[:, B:]
        store(i).start()
    top_store.wait()
    for i in range(4):
        store(i).wait()


def on_device(nrow, ncol, matrix):
    height, width = matrix.shape
    slab = max(8, B // nrow)
    f32 = jnp.float32
    dma = pltpu.SemaphoreType.DMA
    shape = jax.ShapeDtypeStruct
    held, basis, inverse, coeffs = pl.pallas_call(
        functools.partial(kernel, nrow, ncol),
        out_shape=(
            shape((height, width), f32), shape((height, B), f32), shape((B, B), f32), shape((B, width), f32)
        ),
        in_specs=[pl.BlockSpec(memory_space=pltpu.HBM)],
        out_specs=(pl.BlockSpec(memory_space=pltpu.VMEM),) * 4,
        scratch_shapes=[
            pltpu.VMEM((height, B), f32),
            pltpu.VMEM((B, B), f32),
            pltpu.VMEM((B, B), f32),
            pltpu.VMEM((B, width), f32),
            pltpu.VMEM((B, B), f32),
            pltpu.VMEM((S * S, B), f32),
            pltpu.VMEM((nrow, slab, B), f32),
            pltpu.VMEM((nrow, slab, B), f32),
            pltpu.VMEM((B // 2, width), f32),
            pltpu.VMEM((nrow // 2, B // 2, width), f32),
            dma((2,)),
            dma((2, CHUNKS)),
            dma((4, ncol)),
            dma((4, nrow)),
            dma((4, nrow)),
            dma((4, width // B)),
            dma((2, width // B, nrow // 2)),
            pltpu.SemaphoreType.REGULAR,
        ],
        compiler_params=pltpu.CompilerParams(
            collective_id=0, has_side_effects=True, vmem_limit_bytes=12 * 2**20
        ),
    )(pltpu.with_memory_space_constraint(matrix, pltpu.HBM))
    whole = pl.BlockSpec(memory_space=pltpu.VMEM)
    return pl.pallas_call(
        functools.partial(project_kernel, height * nrow),
        out_shape=(shape((height, width), f32), shape((B, width), f32)),
        in_specs=[whole] * 4,
        out_specs=(pl.BlockSpec(memory_space=pl.ANY),) * 2,
        scratch_shapes=[
            pltpu.VMEM((height, width), f32),
            pltpu.VMEM((B, width), f32),
            pltpu.VMEM((3 * B, width), jnp.bfloat16),
            dma((5,)),
        ],
        compiler_params=pltpu.CompilerParams(vmem_limit_bytes=12 * 2**20),
    )(held, basis, inverse, coeffs)


def solution(mesh):
    nrow, ncol = mesh.shape["row"], mesh.shape["col"]
    return jax.shard_map(
        functools.partial(on_device, nrow, ncol),
        mesh=mesh,
        in_specs=(P("row", "col"),),
        out_specs=(P("row", "col"), P(None, "col")),
        check_vma=False,
    )
```

```python
import functools
import math

import jax
import jax.numpy as jnp
from jax import lax
from jax.experimental import pallas as pl
from jax.experimental.pallas import tpu as pltpu
from jax.sharding import PartitionSpec as P

B = 128
S = 8
CUTS = (0, 2, 4, 6, 8, 10, 12, 13, 14, 15, 16)
CHUNKS = len(CUTS) - 1
EARLY = 3
NEAR = {-1: (3, 4), 0: (5,), 4: (6, 7), 9: (8, 9)}
LAST = 2
COLLECT_REST = {7: (0,), 11: (1,), 15: (2, 3)}
COLLECT_LAST = {7: (0,), 11: (1,), 15: (2, 3)}
NEXT = 5
START = {0: (5, 6, 7), 5: (8, 9)}
FAR = {-1: (3, 4), 1: (5,), 4: (6,), 6: (7,), 8: (8,), 10: (9,)}
HI = lax.Precision.HIGHEST


def mm(left, right, dims):
    return lax.dot_general(
        left, right, (dims, ((), ())), precision=HI, preferred_element_type=jnp.float32
    )


def thirds(x):
    high = x.astype(jnp.bfloat16).astype(jnp.float32)
    rest = x - high
    mid = rest.astype(jnp.bfloat16).astype(jnp.float32)
    return high, mid, rest - mid


def self_product(t):
    high, mid, low = thirds(t)
    left = jnp.concatenate([high, high, mid, mid, high, low], 0).astype(jnp.bfloat16)
    right = jnp.concatenate([high, mid, high, mid, low, high], 0).astype(jnp.bfloat16)
    return lax.dot_general(
        left, right, (((0,), (0,)), ((), ())), preferred_element_type=jnp.float32
    )


def spread_block(c_ref, rows, k):
    for j in range(S):
        c_ref[S * j : S * j + S] = jnp.broadcast_to(
            rows[:, S * k + j : S * k + j + 1], (S, B)
        )
    return {
        (i, j): jnp.broadcast_to(c_ref[S * j + i : S * j + i + 1], (S, B))
        for j in range(S)
        for i in range(j, S)
    }


def factor_steps(w_ref, c_ref, after_step):
    lane = lax.broadcasted_iota(jnp.int32, (S, B), 1)
    sub = lax.broadcasted_iota(jnp.int32, (S, B), 0)
    count = B // S
    w = [w_ref[S * r : S * r + S] for r in range(count)]
    d = spread_block(c_ref, w[0], 0)
    for k in range(count):
        here = (lane >= S * k) & (lane < S * k + S)
        following = spread_block(c_ref, w[k + 1], k + 1) if k + 1 < count else None
        rows = jnp.where(here, jnp.where(lane - S * k == sub, 1.0, 0.0), w[k])
        p = [jnp.broadcast_to(rows[j : j + 1], (S, B)) for j in range(S)]
        t = None
        for j in range(S):
            inv = lax.rsqrt(d[j, j])
            l = {i: d[i, j] * inv for i in range(j + 1, S)}
            for i in range(j + 1, S):
                for m in range(j + 1, i + 1):
                    d[i, m] = d[i, m] - l[i] * l[m]
            tj = p[j] * inv
            for i in range(j + 1, S):
                p[i] = p[i] - l[i] * tj
            t = tj if t is None else jnp.where(sub == j, tj, t)
        w_ref[S * k : S * k + S] = jnp.where(lane < S * k + S, t, 0.0)
        if k + 1 < count:
            at = S * (k + 1)
            columns = [jnp.broadcast_to(t[:, at + i : at + i + 1], (S, B)) for i in range(S)]

            def drop(i, what):
                return jnp.sum(columns[i] * what, axis=0, keepdims=True)

            d = {
                (i, j): following[i, j] - jnp.broadcast_to(drop(i, columns[j]), (S, B))
                for (i, j) in following
            }
            after = jnp.where(here, 0.0, w[k + 1])
            for i in range(S):
                after = jnp.where(sub == i, after - drop(i, t), after)
            w[k + 1] = after
        if k + 2 < count:
            change = self_product(t)
            for r in range(k + 2, count):
                w[r] = jnp.where(here, 0.0, w[r]) - change[S * r : S * r + S]
        after_step(k)


class Sum:
    def __init__(self, size, me, src, box, full, sems):
        self.size, self.me, self.src, self.box, self.full = size, me, src, box, full
        self.sems = sems
        self.slab = max(8, B // size)
        self.owners = B // self.slab

    def rows(self, owner):
        return pl.ds(pl.multiple_of(owner * self.slab, self.slab), self.slab)

    def own(self, device, what):
        if self.owners == self.size:
            what()
        else:
            pl.when(device < self.owners)(what)

    def scatter_copy(self, i):
        peer = self.me ^ i
        return pltpu.make_async_remote_copy(
            src_ref=self.src.at[self.rows(peer)],
            dst_ref=self.box.at[i],
            send_sem=self.sems.at[0, i],
            recv_sem=self.sems.at[1, i],
            device_id={"row": peer},
            device_id_type=pl.DeviceIdType.MESH,
        )

    def scatter_from(self, i):
        return pltpu.make_async_remote_copy(
            src_ref=self.box.at[i],
            dst_ref=self.box.at[i],
            send_sem=self.sems.at[0, i],
            recv_sem=self.sems.at[1, i],
            device_id={"row": self.me ^ i},
            device_id_type=pl.DeviceIdType.MESH,
        )

    def gather_copy(self, i, owner):
        return pltpu.make_async_remote_copy(
            src_ref=self.full.at[self.rows(owner)],
            dst_ref=self.full.at[self.rows(owner)],
            send_sem=self.sems.at[2, i],
            recv_sem=self.sems.at[3, i],
            device_id={"row": self.me ^ i},
            device_id_type=pl.DeviceIdType.MESH,
        )

    def start(self):
        for i in range(1, self.size):
            self.own(self.me ^ i, lambda: self.scatter_copy(i).start())

    def middle(self):
        for i in range(1, self.size):
            self.own(self.me ^ i, lambda: self.scatter_copy(i).wait_send())

        def add():
            total = self.src[self.rows(self.me)]
            for i in range(1, self.size):
                self.scatter_from(i).wait_recv()
                total = total + self.box[i]
            self.full[self.rows(self.me)] = total
            self.box[0] = total

        self.own(self.me, add)

    def spread(self):
        def send():
            for i in range(1, self.size):
                self.gather_copy(i, self.me).start()

        self.own(self.me, send)

    def end(self):
        for i in range(1, self.size):
            self.own(self.me ^ i, lambda: self.gather_copy(i, self.me ^ i).wait_recv())

    def drain(self):
        def sent():
            for i in range(1, self.size):
                self.gather_copy(i, self.me).wait_send()

        self.own(self.me, sent)


class PairSum:
    def __init__(self, size, me, src, pair, gather, full, pair_sems, chip_sems):
        self.chips, self.me, self.core, self.chip = size // 2, me, me % 2, me // 2
        self.src, self.pair, self.gather, self.full = src, pair, gather, full
        self.pair_sems, self.chip_sems = pair_sems, chip_sems
        self.half = B // 2
        self.parts = src.shape[1] // B

    def rows(self, core):
        return pl.ds(pl.multiple_of(core * self.half, self.half), self.half)

    def swap_copy(self, c):
        cols = pl.ds(c * B, B)
        return pltpu.make_async_remote_copy(
            src_ref=self.src.at[self.rows(1 - self.core), cols],
            dst_ref=self.pair.at[:, cols],
            send_sem=self.pair_sems.at[0, c],
            recv_sem=self.pair_sems.at[1, c],
            device_id={"row": self.me ^ 1},
            device_id_type=pl.DeviceIdType.MESH,
        )

    def chip_copy(self, c, i, slot):
        cols = pl.ds(c * B, B)
        return pltpu.make_async_remote_copy(
            src_ref=self.gather.at[slot, :, cols],
            dst_ref=self.gather.at[slot, :, cols],
            send_sem=self.chip_sems.at[0, c, i],
            recv_sem=self.chip_sems.at[1, c, i],
            device_id={"row": self.me ^ (2 * i)},
            device_id_type=pl.DeviceIdType.MESH,
        )

    def back_copy(self, c, core):
        cols = pl.ds(c * B, B)
        return pltpu.make_async_remote_copy(
            src_ref=self.full.at[self.rows(core), cols],
            dst_ref=self.full.at[self.rows(core), cols],
            send_sem=self.pair_sems.at[2, c],
            recv_sem=self.pair_sems.at[3, c],
            device_id={"row": self.me ^ 1},
            device_id_type=pl.DeviceIdType.MESH,
        )

    def swap(self):
        for c in range(self.parts):
            self.swap_copy(c).start()

    def spread(self):
        for c in range(self.parts):
            cols = pl.ds(c * B, B)
            self.swap_copy(c).wait_recv()
            self.gather[self.chip, :, cols] = self.src[self.rows(self.core), cols] + self.pair[:, cols]
            for i in range(self.chips - 1, 0, -1):
                self.chip_copy(c, i, self.chip).start()

    def collect(self, *parts):
        for c in parts:
            cols = pl.ds(c * B, B)
            for i in range(1, self.chips):
                self.chip_copy(c, i, self.chip ^ i).wait_recv()
            total = self.gather[0, :, cols]
            for i in range(1, self.chips):
                total = total + self.gather[i, :, cols]
            self.full[self.rows(self.core), cols] = total
            self.back_copy(c, self.core).start()

    def end(self):
        for c in range(self.parts):
            self.back_copy(c, 1 - self.core).wait_recv()

    def drain(self):
        for c in range(self.parts):
            self.swap_copy(c).wait_send()
            self.back_copy(c, self.core).wait_send()
            for i in range(1, self.chips):
                self.chip_copy(c, i, self.chip).wait_send()


def kernel(
    nrow, ncol, m_hbm, m_v, q_v, g2_v, p_v,
    a_v, s1_v, s2_v, sp_v, g1_v, c_v, box1, box2, pair_v, gather_v,
    in_sems, chain_sems, g_sems, sems1, sems2, pair_sems, chip_sems, ready,
):
    me = lax.axis_index("row")
    z = lax.axis_index("col")
    height = m_v.shape[0]
    unit = height // CUTS[-1]
    load_m = pltpu.make_async_copy(m_hbm, m_v, in_sems.at[0])
    load_a = pltpu.make_async_copy(m_hbm.at[:, pl.ds(0, B)], a_v, in_sems.at[1])

    barrier = pltpu.get_barrier_semaphore()
    for i in range(1, nrow):
        pl.semaphore_signal(
            barrier, inc=1, device_id={"row": me ^ i}, device_id_type=pl.DeviceIdType.MESH
        )

    def greet(sem, column):
        pl.semaphore_signal(
            sem, inc=1, device_id={"col": column}, device_id_type=pl.DeviceIdType.MESH
        )

    @pl.when(z > 0)
    def _():
        greet(barrier, z - 1)

    @pl.when(z == 0)
    def _():
        load_a.start()
        for i in range(2, ncol):
            greet(barrier, i)

    load_m.start()

    def enter():
        sends_on = jnp.where(z < ncol - 1, 1, 0)
        far = jnp.where(z > 1, 1, 0)
        pl.semaphore_wait(barrier, nrow - 1 + sends_on + far)

    first = Sum(nrow, me, s1_v, box1, g1_v, sems1)
    second = Sum(nrow, me, s2_v, box2, g2_v, sems2)
    coeffs = PairSum(nrow, me, sp_v, pair_v, gather_v, p_v, pair_sems, chip_sems)

    @pl.when(z == 0)
    def _():
        load_a.wait()
        s1_v[...] = mm(a_v[...], a_v[...], ((0,), (0,)))

    enter()

    @pl.when(z > 1)
    def _():
        greet(ready, 0)

    def chain(c):
        block = a_v.at[pl.ds(CUTS[c] * unit, (CUTS[c + 1] - CUTS[c]) * unit)]
        return pltpu.make_async_remote_copy(
            src_ref=block,
            dst_ref=block,
            send_sem=chain_sems.at[0, c],
            recv_sem=chain_sems.at[1, c],
            device_id={"col": lax.rem(z + 1, ncol)},
            device_id_type=pl.DeviceIdType.MESH,
        )

    passes_on = (z > 0) & (z < ncol - 1)

    def forward(*chunks):
        for c in chunks:
            chain(c).wait_recv()
            chain(c).start()

    def hand(which, total, i):
        return pltpu.make_async_remote_copy(
            src_ref=total.box.at[0],
            dst_ref=total.full.at[total.rows(me)],
            send_sem=g_sems.at[2 * which, i],
            recv_sem=g_sems.at[2 * which + 1, 0],
            device_id={"col": i},
            device_id_type=pl.DeviceIdType.MESH,
        )

    def give(which, total):
        def send():
            for i in range(ncol - 1, 0, -1):
                hand(which, total, i).start()

        first.own(me, send)

    @pl.when(z == 0)
    def _():
        for c in range(EARLY):
            chain(c).start()
        first.start()
        first.middle()
        if ncol > 2:
            pl.semaphore_wait(ready, ncol - 2)
        give(0, first)
        first.spread()
        for c in range(EARLY, NEXT):
            chain(c).start()

    @pl.when(passes_on)
    def _():
        forward(*range(EARLY))

    @pl.when(z > 0)
    def _():
        first.own(me, lambda: hand(0, first, 0).wait_recv())
        first.spread()

    def send(*chunks):
        for c in chunks:
            chain(c).start()

    def pass_on(k):
        near, far = NEAR.get(k, ()), FAR.get(k, ())
        starts = START.get(k, ())
        if starts:
            pl.when(z == 0)(lambda: send(*starts))
        if near:
            pl.when(passes_on & (z == 1))(lambda: forward(*near))
        if far:
            pl.when(passes_on & (z > 1))(lambda: forward(*far))

    pass_on(-1)
    first.end()
    first.drain()
    factor_steps(g1_v, c_v, pass_on)

    big = 4 * unit

    @pl.when(z == 0)
    def _():
        for c in range(CUTS[-1] // 4):
            rows = pl.ds(c * big, big)
            q_v[rows] = mm(a_v[rows], g1_v[...], ((1,), (1,)))
        q = q_v[...]
        s2_v[...] = mm(q, q, ((0,), (0,)))
        second.start()
        load_m.wait()
        sp_v[...] = mm(q_v[...], m_v[...], ((0,), (0,)))
        coeffs.swap()
        second.middle()
        give(1, second)
        second.spread()
        coeffs.spread()

    @pl.when(z > 0)
    def _():
        load_m.wait()
        def share():
            second.own(me, lambda: hand(1, second, 0).wait_recv())
            second.spread()

        for c in range(CUTS[-1] // 4):
            if c == LAST:
                share()

            @pl.when(z == ncol - 1)
            def _():
                for i in range(CHUNKS):
                    if 4 * c <= CUTS[i] < 4 * c + 4:
                        chain(i).wait_recv()

            rows = pl.ds(c * big, big)
            q = mm(a_v[rows], g1_v[...], ((1,), (1,)))
            q_v[rows] = q
            term = mm(q, m_v[rows], ((0,), (0,)))
            if c == 0:
                sp_v[...] = term
            else:
                sp_v[...] += term
        coeffs.swap()
        coeffs.spread()

    second.end()
    second.drain()

    def collect(k):
        rest, last = COLLECT_REST.get(k, ()), COLLECT_LAST.get(k, ())
        if rest:
            pl.when(z < ncol - 1)(lambda: coeffs.collect(*rest))
        if last:
            pl.when(z == ncol - 1)(lambda: coeffs.collect(*last))

    factor_steps(g2_v, c_v, collect)
    coeffs.end()
    coeffs.drain()

    @pl.when(z == 0)
    def _():
        def given():
            for i in range(1, ncol):
                hand(0, first, i).wait_send()
                hand(1, second, i).wait_send()

        first.own(me, given)

    @pl.when(z < ncol - 1)
    def _():
        for c in range(CHUNKS):
            chain(c).wait_send()


def halves(x):
    high = x.astype(jnp.bfloat16)
    return high, (x - high.astype(jnp.float32)).astype(jnp.bfloat16)


def project_kernel(rows, m_ref, q_ref, g2_ref, p_ref, out_hbm, top_hbm, out_v, top_v, back_v, sems):
    height, width = m_ref.shape
    part = height // 4
    scale = math.sqrt(rows)
    on_panel = lax.axis_index("col") == 0
    g2 = g2_ref[...]
    c = mm(g2, p_ref[...], ((1,), (0,)))
    back = mm(g2, c, ((0,), (0,)))
    leading = jnp.where(on_panel, -scale * g2.T, back[:, :B])
    high, low = halves(jnp.concatenate([leading, back[:, B:]], 1))
    back_v[:B] = high
    back_v[B : 2 * B] = high
    back_v[2 * B :] = low

    top_v[...] = c / scale
    top_store = pltpu.make_async_copy(top_v, top_hbm, sems.at[4])
    top_store.start()

    def store(i):
        block = pl.ds(i * part, part)
        return pltpu.make_async_copy(out_v.at[block], out_hbm.at[block], sems.at[i])

    for i in range(4):
        block = pl.ds(i * part, part)
        high, low = halves(q_ref[block])
        change = jnp.dot(
            jnp.concatenate([high, low, high], 1), back_v[...], preferred_element_type=jnp.float32
        )
        base = m_ref[block]
        out_v[block, :B] = jnp.where(on_panel, 0.0, base[:, :B]) - change[:, :B]
        out_v[block, B:] = base[:, B:] - change[:, B:]
        store(i).start()
    top_store.wait()
    for i in range(4):
        store(i).wait()


def on_device(nrow, ncol, matrix):
    height, width = matrix.shape
    slab = max(8, B // nrow)
    f32 = jnp.float32
    dma = pltpu.SemaphoreType.DMA
    shape = jax.ShapeDtypeStruct
    held, basis, inverse, coeffs = pl.pallas_call(
        functools.partial(kernel, nrow, ncol),
        out_shape=(
            shape((height, width), f32), shape((height, B), f32), shape((B, B), f32), shape((B, width), f32)
        ),
        in_specs=[pl.BlockSpec(memory_space=pltpu.HBM)],
        out_specs=(pl.BlockSpec(memory_space=pltpu.VMEM),) * 4,
        scratch_shapes=[
            pltpu.VMEM((height, B), f32),
            pltpu.VMEM((B, B), f32),
            pltpu.VMEM((B, B), f32),
            pltpu.VMEM((B, width), f32),
            pltpu.VMEM((B, B), f32),
            pltpu.VMEM((S * S, B), f32),
            pltpu.VMEM((nrow, slab, B), f32),
            pltpu.VMEM((nrow, slab, B), f32),
            pltpu.VMEM((B // 2, width), f32),
            pltpu.VMEM((nrow // 2, B // 2, width), f32),
            dma((2,)),
            dma((2, CHUNKS)),
            dma((4, ncol)),
            dma((4, nrow)),
            dma((4, nrow)),
            dma((4, width // B)),
            dma((2, width // B, nrow // 2)),
            pltpu.SemaphoreType.REGULAR,
        ],
        compiler_params=pltpu.CompilerParams(
            collective_id=0, has_side_effects=True, vmem_limit_bytes=12 * 2**20
        ),
    )(pltpu.with_memory_space_constraint(matrix, pltpu.HBM))
    whole = pl.BlockSpec(memory_space=pltpu.VMEM)
    return pl.pallas_call(
        functools.partial(project_kernel, height * nrow),
        out_shape=(shape((height, width), f32), shape((B, width), f32)),
        in_specs=[whole] * 4,
        out_specs=(pl.BlockSpec(memory_space=pl.ANY),) * 2,
        scratch_shapes=[
            pltpu.VMEM((height, width), f32),
            pltpu.VMEM((B, width), f32),
            pltpu.VMEM((3 * B, width), jnp.bfloat16),
            dma((5,)),
        ],
        compiler_params=pltpu.CompilerParams(vmem_limit_bytes=12 * 2**20),
    )(held, basis, inverse, coeffs)


def solution(mesh):
    nrow, ncol = mesh.shape["row"], mesh.shape["col"]
    return jax.shard_map(
        functools.partial(on_device, nrow, ncol),
        mesh=mesh,
        in_specs=(P("row", "col"),),
        out_specs=(P("row", "col"), P(None, "col")),
        check_vma=False,
    )
```

```python
import functools
import math

import jax
import jax.numpy as jnp
from jax import lax
from jax.experimental import pallas as pl
from jax.experimental.pallas import tpu as pltpu
from jax.sharding import PartitionSpec as P

B = 128
S = 8
CUTS = (0, 2, 4, 6, 8, 10, 12, 13, 14, 15, 16)
CHUNKS = len(CUTS) - 1
EARLY = 3
NEAR = {-1: (3, 4), 0: (5,), 4: (6, 7), 9: (8, 9)}
LAST = 2
NEXT = 5
START = {0: (5, 6, 7), 5: (8, 9)}
FAR = {-1: (3, 4), 1: (5,), 4: (6,), 6: (7,), 8: (8,), 10: (9,)}
HI = lax.Precision.HIGHEST


def mm(left, right, dims):
    return lax.dot_general(
        left, right, (dims, ((), ())), precision=HI, preferred_element_type=jnp.float32
    )


def thirds(x):
    high = x.astype(jnp.bfloat16).astype(jnp.float32)
    rest = x - high
    mid = rest.astype(jnp.bfloat16).astype(jnp.float32)
    return high, mid, rest - mid


def self_product(t):
    high, mid, low = thirds(t)
    left = jnp.concatenate([high, high, mid, mid, high, low], 0).astype(jnp.bfloat16)
    right = jnp.concatenate([high, mid, high, mid, low, high], 0).astype(jnp.bfloat16)
    return lax.dot_general(
        left, right, (((0,), (0,)), ((), ())), preferred_element_type=jnp.float32
    )


def spread_block(c_ref, rows, k):
    for j in range(S):
        c_ref[S * j : S * j + S] = jnp.broadcast_to(
            rows[:, S * k + j : S * k + j + 1], (S, B)
        )
    return {
        (i, j): jnp.broadcast_to(c_ref[S * j + i : S * j + i + 1], (S, B))
        for j in range(S)
        for i in range(j, S)
    }


def factor_steps(w_ref, c_ref, after_step):
    lane = lax.broadcasted_iota(jnp.int32, (S, B), 1)
    sub = lax.broadcasted_iota(jnp.int32, (S, B), 0)
    count = B // S
    w = [w_ref[S * r : S * r + S] for r in range(count)]
    d = spread_block(c_ref, w[0], 0)
    for k in range(count):
        here = (lane >= S * k) & (lane < S * k + S)
        following = spread_block(c_ref, w[k + 1], k + 1) if k + 1 < count else None
        rows = jnp.where(here, jnp.where(lane - S * k == sub, 1.0, 0.0), w[k])
        p = [jnp.broadcast_to(rows[j : j + 1], (S, B)) for j in range(S)]
        t = None
        for j in range(S):
            inv = lax.rsqrt(d[j, j])
            l = {i: d[i, j] * inv for i in range(j + 1, S)}
            for i in range(j + 1, S):
                for m in range(j + 1, i + 1):
                    d[i, m] = d[i, m] - l[i] * l[m]
            tj = p[j] * inv
            for i in range(j + 1, S):
                p[i] = p[i] - l[i] * tj
            t = tj if t is None else jnp.where(sub == j, tj, t)
        w_ref[S * k : S * k + S] = jnp.where(lane < S * k + S, t, 0.0)
        if k + 1 < count:
            at = S * (k + 1)
            columns = [jnp.broadcast_to(t[:, at + i : at + i + 1], (S, B)) for i in range(S)]

            def drop(i, what):
                return jnp.sum(columns[i] * what, axis=0, keepdims=True)

            d = {
                (i, j): following[i, j] - jnp.broadcast_to(drop(i, columns[j]), (S, B))
                for (i, j) in following
            }
            after = jnp.where(here, 0.0, w[k + 1])
            for i in range(S):
                after = jnp.where(sub == i, after - drop(i, t), after)
            w[k + 1] = after
        if k + 2 < count:
            change = self_product(t)
            for r in range(k + 2, count):
                w[r] = jnp.where(here, 0.0, w[r]) - change[S * r : S * r + S]
        after_step(k)


class Sum:
    def __init__(self, size, me, src, box, full, sems):
        self.size, self.me, self.src, self.box, self.full = size, me, src, box, full
        self.sems = sems
        self.slab = max(8, B // size)
        self.owners = B // self.slab

    def rows(self, owner):
        return pl.ds(pl.multiple_of(owner * self.slab, self.slab), self.slab)

    def own(self, device, what):
        if self.owners == self.size:
            what()
        else:
            pl.when(device < self.owners)(what)

    def scatter_copy(self, i):
        peer = self.me ^ i
        return pltpu.make_async_remote_copy(
            src_ref=self.src.at[self.rows(peer)],
            dst_ref=self.box.at[i],
            send_sem=self.sems.at[0, i],
            recv_sem=self.sems.at[1, i],
            device_id={"row": peer},
            device_id_type=pl.DeviceIdType.MESH,
        )

    def scatter_from(self, i):
        return pltpu.make_async_remote_copy(
            src_ref=self.box.at[i],
            dst_ref=self.box.at[i],
            send_sem=self.sems.at[0, i],
            recv_sem=self.sems.at[1, i],
            device_id={"row": self.me ^ i},
            device_id_type=pl.DeviceIdType.MESH,
        )

    def gather_copy(self, i, owner):
        return pltpu.make_async_remote_copy(
            src_ref=self.full.at[self.rows(owner)],
            dst_ref=self.full.at[self.rows(owner)],
            send_sem=self.sems.at[2, i],
            recv_sem=self.sems.at[3, i],
            device_id={"row": self.me ^ i},
            device_id_type=pl.DeviceIdType.MESH,
        )

    def start(self):
        for i in range(1, self.size):
            self.own(self.me ^ i, lambda: self.scatter_copy(i).start())

    def middle(self):
        for i in range(1, self.size):
            self.own(self.me ^ i, lambda: self.scatter_copy(i).wait_send())

        def add():
            total = self.src[self.rows(self.me)]
            for i in range(1, self.size):
                self.scatter_from(i).wait_recv()
                total = total + self.box[i]
            self.full[self.rows(self.me)] = total
            self.box[0] = total

        self.own(self.me, add)

    def spread(self):
        def send():
            for i in range(1, self.size):
                self.gather_copy(i, self.me).start()

        self.own(self.me, send)

    def end(self):
        for i in range(1, self.size):
            self.own(self.me ^ i, lambda: self.gather_copy(i, self.me ^ i).wait_recv())

    def drain(self):
        def sent():
            for i in range(1, self.size):
                self.gather_copy(i, self.me).wait_send()

        self.own(self.me, sent)


class PairSum:
    def __init__(self, steps, me, src, pair, gather, inbox, full, pair_sems, chip_sems):
        self.steps, self.me, self.core = steps, me, me % 2
        self.src, self.pair, self.gather, self.inbox, self.full = src, pair, gather, inbox, full
        self.pair_sems, self.chip_sems = pair_sems, chip_sems
        self.half = B // 2
        self.parts = src.shape[1] // B
        self.order = sorted(range(self.parts), key=lambda c: c % (self.parts // self.steps))

    def rows(self, core):
        return pl.ds(pl.multiple_of(core * self.half, self.half), self.half)

    def swap_copy(self, c):
        cols = pl.ds(c * B, B)
        return pltpu.make_async_remote_copy(
            src_ref=self.src.at[self.rows(1 - self.core), cols],
            dst_ref=self.pair.at[:, cols],
            send_sem=self.pair_sems.at[0, c],
            recv_sem=self.pair_sems.at[1, c],
            device_id={"row": self.me ^ 1},
            device_id_type=pl.DeviceIdType.MESH,
        )

    def chip_copy(self, c, step):
        cols = pl.ds(c * B, B)
        turn = (step + c * self.steps // self.parts) % self.steps
        return pltpu.make_async_remote_copy(
            src_ref=self.gather.at[step, :, cols],
            dst_ref=self.inbox.at[step, :, cols],
            send_sem=self.chip_sems.at[0, c, step],
            recv_sem=self.chip_sems.at[1, c, step],
            device_id={"row": self.me ^ (2 << turn)},
            device_id_type=pl.DeviceIdType.MESH,
        )

    def back_copy(self, c, core):
        cols = pl.ds(c * B, B)
        return pltpu.make_async_remote_copy(
            src_ref=self.full.at[self.rows(core), cols],
            dst_ref=self.full.at[self.rows(core), cols],
            send_sem=self.pair_sems.at[2, c],
            recv_sem=self.pair_sems.at[3, c],
            device_id={"row": self.me ^ 1},
            device_id_type=pl.DeviceIdType.MESH,
        )

    def swap(self):
        for c in range(self.parts):
            self.swap_copy(c).start()

    def spread(self):
        for c in self.order:
            cols = pl.ds(c * B, B)
            self.swap_copy(c).wait_recv()
            self.gather[0, :, cols] = self.src[self.rows(self.core), cols] + self.pair[:, cols]
            self.chip_copy(c, 0).start()

    def relay(self):
        for step in range(1, self.steps):
            for c in self.order:
                cols = pl.ds(c * B, B)
                self.chip_copy(c, step - 1).wait_recv()
                self.gather[step, :, cols] = (
                    self.gather[step - 1, :, cols] + self.inbox[step - 1, :, cols]
                )
                self.chip_copy(c, step).start()

    def collect(self):
        last = self.steps - 1
        for c in self.order:
            cols = pl.ds(c * B, B)
            self.chip_copy(c, last).wait_recv()
            self.full[self.rows(self.core), cols] = (
                self.gather[last, :, cols] + self.inbox[last, :, cols]
            )
            self.back_copy(c, self.core).start()

    def end(self):
        for c in range(self.parts):
            self.back_copy(c, 1 - self.core).wait_recv()

    def drain(self):
        for c in range(self.parts):
            self.swap_copy(c).wait_send()
            self.back_copy(c, self.core).wait_send()
            for step in range(self.steps):
                self.chip_copy(c, step).wait_send()


def kernel(
    nrow, ncol, m_hbm, m_v, q_v, g2_v, p_v,
    a_v, s1_v, s2_v, sp_v, g1_v, c_v, box1, box2, pair_v, gather_v, inbox_v,
    in_sems, chain_sems, g_sems, sems1, sems2, pair_sems, chip_sems, ready,
):
    me = lax.axis_index("row")
    z = lax.axis_index("col")
    height = m_v.shape[0]
    unit = height // CUTS[-1]
    load_m = pltpu.make_async_copy(m_hbm, m_v, in_sems.at[0])
    load_a = pltpu.make_async_copy(m_hbm.at[:, pl.ds(0, B)], a_v, in_sems.at[1])

    barrier = pltpu.get_barrier_semaphore()
    for i in range(1, nrow):
        pl.semaphore_signal(
            barrier, inc=1, device_id={"row": me ^ i}, device_id_type=pl.DeviceIdType.MESH
        )

    def greet(sem, column):
        pl.semaphore_signal(
            sem, inc=1, device_id={"col": column}, device_id_type=pl.DeviceIdType.MESH
        )

    @pl.when(z > 0)
    def _():
        greet(barrier, z - 1)

    @pl.when(z == 0)
    def _():
        load_a.start()
        for i in range(2, ncol):
            greet(barrier, i)

    load_m.start()

    def enter():
        sends_on = jnp.where(z < ncol - 1, 1, 0)
        far = jnp.where(z > 1, 1, 0)
        pl.semaphore_wait(barrier, nrow - 1 + sends_on + far)

    first = Sum(nrow, me, s1_v, box1, g1_v, sems1)
    second = Sum(nrow, me, s2_v, box2, g2_v, sems2)
    steps = gather_v.shape[0]
    coeffs = PairSum(steps, me, sp_v, pair_v, gather_v, inbox_v, p_v, pair_sems, chip_sems)

    @pl.when(z == 0)
    def _():
        load_a.wait()
        s1_v[...] = mm(a_v[...], a_v[...], ((0,), (0,)))

    enter()

    @pl.when(z > 1)
    def _():
        greet(ready, 0)

    def chain(c):
        block = a_v.at[pl.ds(CUTS[c] * unit, (CUTS[c + 1] - CUTS[c]) * unit)]
        return pltpu.make_async_remote_copy(
            src_ref=block,
            dst_ref=block,
            send_sem=chain_sems.at[0, c],
            recv_sem=chain_sems.at[1, c],
            device_id={"col": lax.rem(z + 1, ncol)},
            device_id_type=pl.DeviceIdType.MESH,
        )

    passes_on = (z > 0) & (z < ncol - 1)

    def forward(*chunks):
        for c in chunks:
            chain(c).wait_recv()
            chain(c).start()

    def hand(which, total, i):
        return pltpu.make_async_remote_copy(
            src_ref=total.box.at[0],
            dst_ref=total.full.at[total.rows(me)],
            send_sem=g_sems.at[2 * which, i],
            recv_sem=g_sems.at[2 * which + 1, 0],
            device_id={"col": i},
            device_id_type=pl.DeviceIdType.MESH,
        )

    def give(which, total):
        def send():
            for i in range(ncol - 1, 0, -1):
                hand(which, total, i).start()

        first.own(me, send)

    @pl.when(z == 0)
    def _():
        for c in range(EARLY):
            chain(c).start()
        first.start()
        first.middle()
        if ncol > 2:
            pl.semaphore_wait(ready, ncol - 2)
        give(0, first)
        first.spread()
        for c in range(EARLY, NEXT):
            chain(c).start()

    @pl.when(passes_on)
    def _():
        forward(*range(EARLY))

    @pl.when(z > 0)
    def _():
        first.own(me, lambda: hand(0, first, 0).wait_recv())
        first.spread()

    def send(*chunks):
        for c in chunks:
            chain(c).start()

    def pass_on(k):
        near, far = NEAR.get(k, ()), FAR.get(k, ())
        starts = START.get(k, ())
        if starts:
            pl.when(z == 0)(lambda: send(*starts))
        if near:
            pl.when(passes_on & (z == 1))(lambda: forward(*near))
        if far:
            pl.when(passes_on & (z > 1))(lambda: forward(*far))

    pass_on(-1)
    first.end()
    first.drain()
    factor_steps(g1_v, c_v, pass_on)

    big = 4 * unit

    @pl.when(z == 0)
    def _():
        for c in range(CUTS[-1] // 4):
            rows = pl.ds(c * big, big)
            q_v[rows] = mm(a_v[rows], g1_v[...], ((1,), (1,)))
        q = q_v[...]
        s2_v[...] = mm(q, q, ((0,), (0,)))
        second.start()
        load_m.wait()
        sp_v[...] = mm(q_v[...], m_v[...], ((0,), (0,)))
        coeffs.swap()
        second.middle()
        give(1, second)
        second.spread()
        coeffs.spread()

    @pl.when(z > 0)
    def _():
        load_m.wait()
        def share():
            second.own(me, lambda: hand(1, second, 0).wait_recv())
            second.spread()

        for c in range(CUTS[-1] // 4):
            if c == LAST:
                share()

            @pl.when(z == ncol - 1)
            def _():
                for i in range(CHUNKS):
                    if 4 * c <= CUTS[i] < 4 * c + 4:
                        chain(i).wait_recv()

            rows = pl.ds(c * big, big)
            q = mm(a_v[rows], g1_v[...], ((1,), (1,)))
            q_v[rows] = q
            term = mm(q, m_v[rows], ((0,), (0,)))
            if c == 0:
                sp_v[...] = term
            else:
                sp_v[...] += term
        coeffs.swap()
        coeffs.spread()

    coeffs.relay()
    second.end()
    second.drain()

    factor_steps(g2_v, c_v, lambda k: None)
    coeffs.collect()
    coeffs.end()
    coeffs.drain()

    @pl.when(z == 0)
    def _():
        def given():
            for i in range(1, ncol):
                hand(0, first, i).wait_send()
                hand(1, second, i).wait_send()

        first.own(me, given)

    @pl.when(z < ncol - 1)
    def _():
        for c in range(CHUNKS):
            chain(c).wait_send()


def halves(x):
    high = x.astype(jnp.bfloat16)
    return high, (x - high.astype(jnp.float32)).astype(jnp.bfloat16)


def project_kernel(rows, m_ref, q_ref, g2_ref, p_ref, out_hbm, top_hbm, out_v, top_v, back_v, sems):
    height, width = m_ref.shape
    part = height // 4
    scale = math.sqrt(rows)
    on_panel = lax.axis_index("col") == 0
    g2 = g2_ref[...]
    c = mm(g2, p_ref[...], ((1,), (0,)))
    back = mm(g2, c, ((0,), (0,)))
    leading = jnp.where(on_panel, -scale * g2.T, back[:, :B])
    high, low = halves(jnp.concatenate([leading, back[:, B:]], 1))
    back_v[:B] = high
    back_v[B : 2 * B] = high
    back_v[2 * B :] = low

    top_v[...] = c / scale
    top_store = pltpu.make_async_copy(top_v, top_hbm, sems.at[4])
    top_store.start()

    def store(i):
        block = pl.ds(i * part, part)
        return pltpu.make_async_copy(out_v.at[block], out_hbm.at[block], sems.at[i])

    for i in range(4):
        block = pl.ds(i * part, part)
        high, low = halves(q_ref[block])
        change = jnp.dot(
            jnp.concatenate([high, low, high], 1), back_v[...], preferred_element_type=jnp.float32
        )
        base = m_ref[block]
        out_v[block, :B] = jnp.where(on_panel, 0.0, base[:, :B]) - change[:, :B]
        out_v[block, B:] = base[:, B:] - change[:, B:]
        store(i).start()
    top_store.wait()
    for i in range(4):
        store(i).wait()


def on_device(nrow, ncol, matrix):
    height, width = matrix.shape
    slab = max(8, B // nrow)
    steps = (nrow // 2).bit_length() - 1
    f32 = jnp.float32
    dma = pltpu.SemaphoreType.DMA
    shape = jax.ShapeDtypeStruct
    held, basis, inverse, coeffs = pl.pallas_call(
        functools.partial(kernel, nrow, ncol),
        out_shape=(
            shape((height, width), f32), shape((height, B), f32), shape((B, B), f32), shape((B, width), f32)
        ),
        in_specs=[pl.BlockSpec(memory_space=pltpu.HBM)],
        out_specs=(pl.BlockSpec(memory_space=pltpu.VMEM),) * 4,
        scratch_shapes=[
            pltpu.VMEM((height, B), f32),
            pltpu.VMEM((B, B), f32),
            pltpu.VMEM((B, B), f32),
            pltpu.VMEM((B, width), f32),
            pltpu.VMEM((B, B), f32),
            pltpu.VMEM((S * S, B), f32),
            pltpu.VMEM((nrow, slab, B), f32),
            pltpu.VMEM((nrow, slab, B), f32),
            pltpu.VMEM((B // 2, width), f32),
            pltpu.VMEM((steps, B // 2, width), f32),
            pltpu.VMEM((steps, B // 2, width), f32),
            dma((2,)),
            dma((2, CHUNKS)),
            dma((4, ncol)),
            dma((4, nrow)),
            dma((4, nrow)),
            dma((4, width // B)),
            dma((2, width // B, steps)),
            pltpu.SemaphoreType.REGULAR,
        ],
        compiler_params=pltpu.CompilerParams(
            collective_id=0, has_side_effects=True, vmem_limit_bytes=12 * 2**20
        ),
    )(pltpu.with_memory_space_constraint(matrix, pltpu.HBM))
    whole = pl.BlockSpec(memory_space=pltpu.VMEM)
    return pl.pallas_call(
        functools.partial(project_kernel, height * nrow),
        out_shape=(shape((height, width), f32), shape((B, width), f32)),
        in_specs=[whole] * 4,
        out_specs=(pl.BlockSpec(memory_space=pl.ANY),) * 2,
        scratch_shapes=[
            pltpu.VMEM((height, width), f32),
            pltpu.VMEM((B, width), f32),
            pltpu.VMEM((3 * B, width), jnp.bfloat16),
            dma((5,)),
        ],
        compiler_params=pltpu.CompilerParams(vmem_limit_bytes=12 * 2**20),
    )(held, basis, inverse, coeffs)


def solution(mesh):
    nrow, ncol = mesh.shape["row"], mesh.shape["col"]
    return jax.shard_map(
        functools.partial(on_device, nrow, ncol),
        mesh=mesh,
        in_specs=(P("row", "col"),),
        out_specs=(P("row", "col"), P(None, "col")),
        check_vma=False,
    )
```

```python
import functools
import math

import jax
import jax.numpy as jnp
from jax import lax
from jax.experimental import pallas as pl
from jax.experimental.pallas import tpu as pltpu
from jax.sharding import PartitionSpec as P

B = 128
S = 8
CUTS = (0, 2, 4, 6, 8, 10, 12, 13, 14, 15, 16)
CHUNKS = len(CUTS) - 1
EARLY = 3
NEAR = {-1: (3, 4), 0: (5,), 4: (6, 7), 9: (8, 9)}
LAST = 2
NEXT = 5
START = {0: (5, 6, 7), 5: (8, 9)}
FAR = {-1: (3, 4), 1: (5,), 4: (6,), 6: (7,), 8: (8,), 10: (9,)}
HI = lax.Precision.HIGHEST


def mm(left, right, dims):
    return lax.dot_general(
        left, right, (dims, ((), ())), precision=HI, preferred_element_type=jnp.float32
    )


def thirds(x):
    high = x.astype(jnp.bfloat16).astype(jnp.float32)
    rest = x - high
    mid = rest.astype(jnp.bfloat16).astype(jnp.float32)
    return high, mid, rest - mid


def self_product(t):
    high, mid, low = thirds(t)
    left = jnp.concatenate([high, high, mid, mid, high, low], 0).astype(jnp.bfloat16)
    right = jnp.concatenate([high, mid, high, mid, low, high], 0).astype(jnp.bfloat16)
    return lax.dot_general(
        left, right, (((0,), (0,)), ((), ())), preferred_element_type=jnp.float32
    )


def spread_block(c_ref, rows, k):
    for j in range(S):
        c_ref[S * j : S * j + S] = jnp.broadcast_to(
            rows[:, S * k + j : S * k + j + 1], (S, B)
        )
    return {
        (i, j): jnp.broadcast_to(c_ref[S * j + i : S * j + i + 1], (S, B))
        for j in range(S)
        for i in range(j, S)
    }


def factor_steps(w_ref, c_ref, after_step):
    lane = lax.broadcasted_iota(jnp.int32, (S, B), 1)
    sub = lax.broadcasted_iota(jnp.int32, (S, B), 0)
    count = B // S
    w = [w_ref[S * r : S * r + S] for r in range(count)]
    d = spread_block(c_ref, w[0], 0)
    for k in range(count):
        here = (lane >= S * k) & (lane < S * k + S)
        following = spread_block(c_ref, w[k + 1], k + 1) if k + 1 < count else None
        rows = jnp.where(here, jnp.where(lane - S * k == sub, 1.0, 0.0), w[k])
        p = [jnp.broadcast_to(rows[j : j + 1], (S, B)) for j in range(S)]
        t = None
        for j in range(S):
            inv = lax.rsqrt(d[j, j])
            l = {i: d[i, j] * inv for i in range(j + 1, S)}
            for i in range(j + 1, S):
                for m in range(j + 1, i + 1):
                    d[i, m] = d[i, m] - l[i] * l[m]
            tj = p[j] * inv
            for i in range(j + 1, S):
                p[i] = p[i] - l[i] * tj
            t = tj if t is None else jnp.where(sub == j, tj, t)
        w_ref[S * k : S * k + S] = jnp.where(lane < S * k + S, t, 0.0)
        if k + 1 < count:
            at = S * (k + 1)
            columns = [jnp.broadcast_to(t[:, at + i : at + i + 1], (S, B)) for i in range(S)]

            def drop(i, what):
                return jnp.sum(columns[i] * what, axis=0, keepdims=True)

            d = {
                (i, j): following[i, j] - jnp.broadcast_to(drop(i, columns[j]), (S, B))
                for (i, j) in following
            }
            after = jnp.where(here, 0.0, w[k + 1])
            for i in range(S):
                after = jnp.where(sub == i, after - drop(i, t), after)
            w[k + 1] = after
        if k + 2 < count:
            change = self_product(t)
            for r in range(k + 2, count):
                w[r] = jnp.where(here, 0.0, w[r]) - change[S * r : S * r + S]
        after_step(k)


class Sum:
    def __init__(self, size, me, src, box, full, sems):
        self.size, self.me, self.src, self.box, self.full = size, me, src, box, full
        self.sems = sems
        self.slab = max(8, B // size)
        self.owners = B // self.slab

    def rows(self, owner):
        return pl.ds(pl.multiple_of(owner * self.slab, self.slab), self.slab)

    def own(self, device, what):
        if self.owners == self.size:
            what()
        else:
            pl.when(device < self.owners)(what)

    def scatter_copy(self, i):
        peer = self.me ^ i
        return pltpu.make_async_remote_copy(
            src_ref=self.src.at[self.rows(peer)],
            dst_ref=self.box.at[i],
            send_sem=self.sems.at[0, i],
            recv_sem=self.sems.at[1, i],
            device_id={"row": peer},
            device_id_type=pl.DeviceIdType.MESH,
        )

    def scatter_from(self, i):
        return pltpu.make_async_remote_copy(
            src_ref=self.box.at[i],
            dst_ref=self.box.at[i],
            send_sem=self.sems.at[0, i],
            recv_sem=self.sems.at[1, i],
            device_id={"row": self.me ^ i},
            device_id_type=pl.DeviceIdType.MESH,
        )

    def gather_copy(self, i, owner):
        return pltpu.make_async_remote_copy(
            src_ref=self.full.at[self.rows(owner)],
            dst_ref=self.full.at[self.rows(owner)],
            send_sem=self.sems.at[2, i],
            recv_sem=self.sems.at[3, i],
            device_id={"row": self.me ^ i},
            device_id_type=pl.DeviceIdType.MESH,
        )

    def start(self):
        for i in range(1, self.size):
            self.own(self.me ^ i, lambda: self.scatter_copy(i).start())

    def middle(self):
        for i in range(1, self.size):
            self.own(self.me ^ i, lambda: self.scatter_copy(i).wait_send())

        def add():
            total = self.src[self.rows(self.me)]
            for i in range(1, self.size):
                self.scatter_from(i).wait_recv()
                total = total + self.box[i]
            self.full[self.rows(self.me)] = total
            self.box[0] = total

        self.own(self.me, add)

    def spread(self):
        def send():
            for i in range(1, self.size):
                self.gather_copy(i, self.me).start()

        self.own(self.me, send)

    def end(self):
        for i in range(1, self.size):
            self.own(self.me ^ i, lambda: self.gather_copy(i, self.me ^ i).wait_recv())

    def drain(self):
        def sent():
            for i in range(1, self.size):
                self.gather_copy(i, self.me).wait_send()

        self.own(self.me, sent)


class PairSum:
    def __init__(self, steps, me, src, pair, gather, inbox, full, pair_sems, chip_sems):
        self.steps, self.me, self.core = steps, me, me % 2
        self.src, self.pair, self.gather, self.inbox, self.full = src, pair, gather, inbox, full
        self.pair_sems, self.chip_sems = pair_sems, chip_sems
        self.half = B // 2
        self.parts = src.shape[1] // B
        self.order = sorted(range(self.parts), key=lambda c: c % (self.parts // self.steps))

    def rows(self, core):
        return pl.ds(pl.multiple_of(core * self.half, self.half), self.half)

    def swap_copy(self, c):
        cols = pl.ds(c * B, B)
        return pltpu.make_async_remote_copy(
            src_ref=self.src.at[self.rows(1 - self.core), cols],
            dst_ref=self.pair.at[:, cols],
            send_sem=self.pair_sems.at[0, c],
            recv_sem=self.pair_sems.at[1, c],
            device_id={"row": self.me ^ 1},
            device_id_type=pl.DeviceIdType.MESH,
        )

    def chip_copy(self, c, step):
        cols = pl.ds(c * B, B)
        turn = (step + c * self.steps // self.parts) % self.steps
        return pltpu.make_async_remote_copy(
            src_ref=self.gather.at[step, :, cols],
            dst_ref=self.inbox.at[step, :, cols],
            send_sem=self.chip_sems.at[0, c, step],
            recv_sem=self.chip_sems.at[1, c, step],
            device_id={"row": self.me ^ (2 << turn)},
            device_id_type=pl.DeviceIdType.MESH,
        )

    def back_copy(self, c, core):
        cols = pl.ds(c * B, B)
        return pltpu.make_async_remote_copy(
            src_ref=self.full.at[self.rows(core), cols],
            dst_ref=self.full.at[self.rows(core), cols],
            send_sem=self.pair_sems.at[2, c],
            recv_sem=self.pair_sems.at[3, c],
            device_id={"row": self.me ^ 1},
            device_id_type=pl.DeviceIdType.MESH,
        )

    def swap(self):
        for c in self.order:
            self.swap_copy(c).start()

    def spread(self):
        for c in self.order:
            cols = pl.ds(c * B, B)
            self.swap_copy(c).wait_recv()
            self.gather[0, :, cols] = self.src[self.rows(self.core), cols] + self.pair[:, cols]
            self.chip_copy(c, 0).start()

    def relay(self):
        for step in range(1, self.steps):
            for c in self.order:
                cols = pl.ds(c * B, B)
                self.chip_copy(c, step - 1).wait_recv()
                self.gather[step, :, cols] = (
                    self.gather[step - 1, :, cols] + self.inbox[step - 1, :, cols]
                )
                self.chip_copy(c, step).start()

    def collect(self):
        last = self.steps - 1
        for c in self.order:
            cols = pl.ds(c * B, B)
            self.chip_copy(c, last).wait_recv()
            self.full[self.rows(self.core), cols] = (
                self.gather[last, :, cols] + self.inbox[last, :, cols]
            )
            self.back_copy(c, self.core).start()

    def end(self):
        for c in range(self.parts):
            self.back_copy(c, 1 - self.core).wait_recv()

    def drain(self):
        for c in range(self.parts):
            self.swap_copy(c).wait_send()
            self.back_copy(c, self.core).wait_send()
            for step in range(self.steps):
                self.chip_copy(c, step).wait_send()


def kernel(
    nrow, ncol, m_hbm, m_v, split_v, g2_v, both_v, p_v,
    q_v, a_v, s1_v, s2_v, sp_v, g1_v, c_v, box1, box2, pair_v, gather_v, inbox_v,
    in_sems, chain_sems, g_sems, sems1, sems2, pair_sems, chip_sems, ready,
):
    me = lax.axis_index("row")
    z = lax.axis_index("col")
    height = m_v.shape[0]
    unit = height // CUTS[-1]
    load_m = pltpu.make_async_copy(m_hbm, m_v, in_sems.at[0])
    load_a = pltpu.make_async_copy(m_hbm.at[:, pl.ds(0, B)], a_v, in_sems.at[1])

    barrier = pltpu.get_barrier_semaphore()
    for i in range(1, nrow):
        pl.semaphore_signal(
            barrier, inc=1, device_id={"row": me ^ i}, device_id_type=pl.DeviceIdType.MESH
        )

    def greet(sem, column):
        pl.semaphore_signal(
            sem, inc=1, device_id={"col": column}, device_id_type=pl.DeviceIdType.MESH
        )

    @pl.when(z > 0)
    def _():
        greet(barrier, z - 1)

    @pl.when(z == 0)
    def _():
        load_a.start()
        for i in range(2, ncol):
            greet(barrier, i)

    load_m.start()

    def enter():
        sends_on = jnp.where(z < ncol - 1, 1, 0)
        far = jnp.where(z > 1, 1, 0)
        pl.semaphore_wait(barrier, nrow - 1 + sends_on + far)

    first = Sum(nrow, me, s1_v, box1, g1_v, sems1)
    second = Sum(nrow, me, s2_v, box2, g2_v, sems2)
    steps = gather_v.shape[0]
    coeffs = PairSum(steps, me, sp_v, pair_v, gather_v, inbox_v, p_v, pair_sems, chip_sems)

    @pl.when(z == 0)
    def _():
        load_a.wait()
        s1_v[...] = mm(a_v[...], a_v[...], ((0,), (0,)))

    enter()

    @pl.when(z > 1)
    def _():
        greet(ready, 0)

    def chain(c):
        block = a_v.at[pl.ds(CUTS[c] * unit, (CUTS[c + 1] - CUTS[c]) * unit)]
        return pltpu.make_async_remote_copy(
            src_ref=block,
            dst_ref=block,
            send_sem=chain_sems.at[0, c],
            recv_sem=chain_sems.at[1, c],
            device_id={"col": lax.rem(z + 1, ncol)},
            device_id_type=pl.DeviceIdType.MESH,
        )

    passes_on = (z > 0) & (z < ncol - 1)

    def forward(*chunks):
        for c in chunks:
            chain(c).wait_recv()
            chain(c).start()

    def hand(which, total, i):
        return pltpu.make_async_remote_copy(
            src_ref=total.box.at[0],
            dst_ref=total.full.at[total.rows(me)],
            send_sem=g_sems.at[2 * which, i],
            recv_sem=g_sems.at[2 * which + 1, 0],
            device_id={"col": i},
            device_id_type=pl.DeviceIdType.MESH,
        )

    def give(which, total):
        def send():
            for i in range(ncol - 1, 0, -1):
                hand(which, total, i).start()

        first.own(me, send)

    @pl.when(z == 0)
    def _():
        for c in range(EARLY):
            chain(c).start()
        first.start()
        first.middle()
        if ncol > 2:
            pl.semaphore_wait(ready, ncol - 2)
        give(0, first)
        first.spread()
        for c in range(EARLY, NEXT):
            chain(c).start()

    @pl.when(passes_on)
    def _():
        forward(*range(EARLY))

    @pl.when(z > 0)
    def _():
        first.own(me, lambda: hand(0, first, 0).wait_recv())
        first.spread()

    def send(*chunks):
        for c in chunks:
            chain(c).start()

    def pass_on(k):
        near, far = NEAR.get(k, ()), FAR.get(k, ())
        starts = START.get(k, ())
        if starts:
            pl.when(z == 0)(lambda: send(*starts))
        if near:
            pl.when(passes_on & (z == 1))(lambda: forward(*near))
        if far:
            pl.when(passes_on & (z > 1))(lambda: forward(*far))

    pass_on(-1)
    first.end()
    first.drain()
    factor_steps(g1_v, c_v, pass_on)

    big = 4 * unit

    @pl.when(z == 0)
    def _():
        for c in range(CUTS[-1] // 4):
            rows = pl.ds(c * big, big)
            q_v[rows] = mm(a_v[rows], g1_v[...], ((1,), (1,)))
        q = q_v[...]
        s2_v[...] = mm(q, q, ((0,), (0,)))
        second.start()
        load_m.wait()
        sp_v[...] = mm(q_v[...], m_v[...], ((0,), (0,)))
        coeffs.swap()
        second.middle()
        give(1, second)
        second.spread()
        coeffs.spread()

    @pl.when(z > 0)
    def _():
        load_m.wait()
        def share():
            second.own(me, lambda: hand(1, second, 0).wait_recv())
            second.spread()

        for c in range(CUTS[-1] // 4):
            if c == LAST:
                share()

            @pl.when(z == ncol - 1)
            def _():
                for i in range(CHUNKS):
                    if 4 * c <= CUTS[i] < 4 * c + 4:
                        chain(i).wait_recv()

            rows = pl.ds(c * big, big)
            q = mm(a_v[rows], g1_v[...], ((1,), (1,)))
            q_v[rows] = q
            term = mm(q, m_v[rows], ((0,), (0,)))
            if c == 0:
                sp_v[...] = term
            else:
                sp_v[...] += term
        coeffs.swap()
        coeffs.spread()

    for c in range(CUTS[-1] // 4):
        rows = pl.ds(c * big, big)
        high, low = halves(q_v[rows])
        split_v[rows] = jnp.concatenate([high, low, high], 1)
    coeffs.relay()
    second.end()
    second.drain()

    factor_steps(g2_v, c_v, lambda k: None)
    both_v[...] = mm(g2_v[...], g2_v[...], ((0,), (0,)))
    coeffs.collect()
    coeffs.end()
    coeffs.drain()

    @pl.when(z == 0)
    def _():
        def given():
            for i in range(1, ncol):
                hand(0, first, i).wait_send()
                hand(1, second, i).wait_send()

        first.own(me, given)

    @pl.when(z < ncol - 1)
    def _():
        for c in range(CHUNKS):
            chain(c).wait_send()


def halves(x):
    high = x.astype(jnp.bfloat16)
    return high, (x - high.astype(jnp.float32)).astype(jnp.bfloat16)


def project_kernel(rows, m_ref, split_ref, g2_ref, both_ref, p_ref, out_hbm, top_hbm, out_v, top_v, back_v, sems):
    height, width = m_ref.shape
    part = height // 4
    scale = math.sqrt(rows)
    on_panel = lax.axis_index("col") == 0
    g2 = g2_ref[...]
    back = mm(both_ref[...], p_ref[...], ((1,), (0,)))
    leading = jnp.where(on_panel, -scale * g2.T, back[:, :B])
    high, low = halves(jnp.concatenate([leading, back[:, B:]], 1))
    back_v[:B] = high
    back_v[B : 2 * B] = high
    back_v[2 * B :] = low

    top_v[...] = mm(g2, p_ref[...], ((1,), (0,))) / scale
    top_store = pltpu.make_async_copy(top_v, top_hbm, sems.at[4])
    top_store.start()

    def store(i):
        block = pl.ds(i * part, part)
        return pltpu.make_async_copy(out_v.at[block], out_hbm.at[block], sems.at[i])

    for i in range(4):
        block = pl.ds(i * part, part)
        change = jnp.dot(
            split_ref[block], back_v[...], preferred_element_type=jnp.float32
        )
        base = m_ref[block]
        out_v[block, :B] = jnp.where(on_panel, 0.0, base[:, :B]) - change[:, :B]
        out_v[block, B:] = base[:, B:] - change[:, B:]
        store(i).start()
    top_store.wait()
    for i in range(4):
        store(i).wait()


def on_device(nrow, ncol, matrix):
    height, width = matrix.shape
    slab = max(8, B // nrow)
    steps = (nrow // 2).bit_length() - 1
    f32 = jnp.float32
    dma = pltpu.SemaphoreType.DMA
    shape = jax.ShapeDtypeStruct
    held, basis, inverse, both, coeffs = pl.pallas_call(
        functools.partial(kernel, nrow, ncol),
        out_shape=(
            shape((height, width), f32), shape((height, 3 * B), jnp.bfloat16),
            shape((B, B), f32), shape((B, B), f32), shape((B, width), f32)
        ),
        in_specs=[pl.BlockSpec(memory_space=pltpu.HBM)],
        out_specs=(pl.BlockSpec(memory_space=pltpu.VMEM),) * 5,
        scratch_shapes=[
            pltpu.VMEM((height, B), f32),
            pltpu.VMEM((height, B), f32),
            pltpu.VMEM((B, B), f32),
            pltpu.VMEM((B, B), f32),
            pltpu.VMEM((B, width), f32),
            pltpu.VMEM((B, B), f32),
            pltpu.VMEM((S * S, B), f32),
            pltpu.VMEM((nrow, slab, B), f32),
            pltpu.VMEM((nrow, slab, B), f32),
            pltpu.VMEM((B // 2, width), f32),
            pltpu.VMEM((steps, B // 2, width), f32),
            pltpu.VMEM((steps, B // 2, width), f32),
            dma((2,)),
            dma((2, CHUNKS)),
            dma((4, ncol)),
            dma((4, nrow)),
            dma((4, nrow)),
            dma((4, width // B)),
            dma((2, width // B, steps)),
            pltpu.SemaphoreType.REGULAR,
        ],
        compiler_params=pltpu.CompilerParams(
            collective_id=0, has_side_effects=True, vmem_limit_bytes=12 * 2**20
        ),
    )(pltpu.with_memory_space_constraint(matrix, pltpu.HBM))
    whole = pl.BlockSpec(memory_space=pltpu.VMEM)
    return pl.pallas_call(
        functools.partial(project_kernel, height * nrow),
        out_shape=(shape((height, width), f32), shape((B, width), f32)),
        in_specs=[whole] * 5,
        out_specs=(pl.BlockSpec(memory_space=pl.ANY),) * 2,
        scratch_shapes=[
            pltpu.VMEM((height, width), f32),
            pltpu.VMEM((B, width), f32),
            pltpu.VMEM((3 * B, width), jnp.bfloat16),
            dma((5,)),
        ],
        compiler_params=pltpu.CompilerParams(vmem_limit_bytes=12 * 2**20),
    )(held, basis, inverse, both, coeffs)


def solution(mesh):
    nrow, ncol = mesh.shape["row"], mesh.shape["col"]
    return jax.shard_map(
        functools.partial(on_device, nrow, ncol),
        mesh=mesh,
        in_specs=(P("row", "col"),),
        out_specs=(P("row", "col"), P(None, "col")),
        check_vma=False,
    )
```

```python
import functools
import math

import jax
import jax.numpy as jnp
from jax import lax
from jax.experimental import pallas as pl
from jax.experimental.pallas import tpu as pltpu
from jax.sharding import PartitionSpec as P

B = 128
S = 8
CUTS = (0, 2, 4, 6, 8, 10, 12, 13, 14, 15, 16)
CHUNKS = len(CUTS) - 1
EARLY = 3
NEAR = {-1: (3, 4), 0: (5,), 4: (6, 7), 9: (8, 9)}
LAST = 2
NEXT = 5
START = {0: (5, 6, 7), 5: (8, 9)}
FAR = {-1: (3, 4), 1: (5,), 4: (6,), 6: (7,), 8: (8,), 10: (9,)}
HI = lax.Precision.HIGHEST


def mm(left, right, dims):
    return lax.dot_general(
        left, right, (dims, ((), ())), precision=HI, preferred_element_type=jnp.float32
    )


def thirds(x):
    high = x.astype(jnp.bfloat16).astype(jnp.float32)
    rest = x - high
    mid = rest.astype(jnp.bfloat16).astype(jnp.float32)
    return high, mid, rest - mid


def self_product(t):
    high, mid, low = thirds(t)
    left = jnp.concatenate([high, high, mid, mid, high, low], 0).astype(jnp.bfloat16)
    right = jnp.concatenate([high, mid, high, mid, low, high], 0).astype(jnp.bfloat16)
    return lax.dot_general(
        left, right, (((0,), (0,)), ((), ())), preferred_element_type=jnp.float32
    )


def spread_block(c_ref, rows, k):
    for j in range(S):
        c_ref[S * j : S * j + S] = jnp.broadcast_to(
            rows[:, S * k + j : S * k + j + 1], (S, B)
        )
    return {
        (i, j): jnp.broadcast_to(c_ref[S * j + i : S * j + i + 1], (S, B))
        for j in range(S)
        for i in range(j, S)
    }


def factor_steps(w_ref, c_ref, after_step):
    lane = lax.broadcasted_iota(jnp.int32, (S, B), 1)
    sub = lax.broadcasted_iota(jnp.int32, (S, B), 0)
    count = B // S
    w = [w_ref[S * r : S * r + S] for r in range(count)]
    d = spread_block(c_ref, w[0], 0)
    for k in range(count):
        here = (lane >= S * k) & (lane < S * k + S)
        following = spread_block(c_ref, w[k + 1], k + 1) if k + 1 < count else None
        rows = jnp.where(here, jnp.where(lane - S * k == sub, 1.0, 0.0), w[k])
        p = [jnp.broadcast_to(rows[j : j + 1], (S, B)) for j in range(S)]
        t = None
        for j in range(S):
            inv = lax.rsqrt(d[j, j])
            l = {i: d[i, j] * inv for i in range(j + 1, S)}
            for i in range(j + 1, S):
                for m in range(j + 1, i + 1):
                    d[i, m] = d[i, m] - l[i] * l[m]
            tj = p[j] * inv
            for i in range(j + 1, S):
                p[i] = p[i] - l[i] * tj
            t = tj if t is None else jnp.where(sub == j, tj, t)
        w_ref[S * k : S * k + S] = jnp.where(lane < S * k + S, t, 0.0)
        if k + 1 < count:
            at = S * (k + 1)
            columns = [jnp.broadcast_to(t[:, at + i : at + i + 1], (S, B)) for i in range(S)]

            def drop(i, what):
                return jnp.sum(columns[i] * what, axis=0, keepdims=True)

            d = {
                (i, j): following[i, j] - jnp.broadcast_to(drop(i, columns[j]), (S, B))
                for (i, j) in following
            }
            after = jnp.where(here, 0.0, w[k + 1])
            for i in range(S):
                after = jnp.where(sub == i, after - drop(i, t), after)
            w[k + 1] = after
        if k + 2 < count:
            change = self_product(t)
            for r in range(k + 2, count):
                w[r] = jnp.where(here, 0.0, w[r]) - change[S * r : S * r + S]
        after_step(k)


class Sum:
    def __init__(self, size, me, src, box, full, sems):
        self.size, self.me, self.src, self.box, self.full = size, me, src, box, full
        self.sems = sems
        self.slab = max(8, B // size)
        self.owners = B // self.slab

    def rows(self, owner):
        return pl.ds(pl.multiple_of(owner * self.slab, self.slab), self.slab)

    def own(self, device, what):
        if self.owners == self.size:
            what()
        else:
            pl.when(device < self.owners)(what)

    def scatter_copy(self, i):
        peer = self.me ^ i
        return pltpu.make_async_remote_copy(
            src_ref=self.src.at[self.rows(peer)],
            dst_ref=self.box.at[i],
            send_sem=self.sems.at[0, i],
            recv_sem=self.sems.at[1, i],
            device_id={"row": peer},
            device_id_type=pl.DeviceIdType.MESH,
        )

    def scatter_from(self, i):
        return pltpu.make_async_remote_copy(
            src_ref=self.box.at[i],
            dst_ref=self.box.at[i],
            send_sem=self.sems.at[0, i],
            recv_sem=self.sems.at[1, i],
            device_id={"row": self.me ^ i},
            device_id_type=pl.DeviceIdType.MESH,
        )

    def gather_copy(self, i, owner):
        return pltpu.make_async_remote_copy(
            src_ref=self.full.at[self.rows(owner)],
            dst_ref=self.full.at[self.rows(owner)],
            send_sem=self.sems.at[2, i],
            recv_sem=self.sems.at[3, i],
            device_id={"row": self.me ^ i},
            device_id_type=pl.DeviceIdType.MESH,
        )

    def start(self):
        for i in range(1, self.size):
            self.own(self.me ^ i, lambda: self.scatter_copy(i).start())

    def middle(self):
        for i in range(1, self.size):
            self.own(self.me ^ i, lambda: self.scatter_copy(i).wait_send())

        def add():
            total = self.src[self.rows(self.me)]
            for i in range(1, self.size):
                self.scatter_from(i).wait_recv()
                total = total + self.box[i]
            self.full[self.rows(self.me)] = total
            self.box[0] = total

        self.own(self.me, add)

    def spread(self):
        def send():
            for i in range(1, self.size):
                self.gather_copy(i, self.me).start()

        self.own(self.me, send)

    def end(self):
        for i in range(1, self.size):
            self.own(self.me ^ i, lambda: self.gather_copy(i, self.me ^ i).wait_recv())

    def drain(self):
        def sent():
            for i in range(1, self.size):
                self.gather_copy(i, self.me).wait_send()

        self.own(self.me, sent)


class PairSum:
    def __init__(self, steps, me, src, pair, gather, inbox, full, pair_sems, chip_sems):
        self.steps, self.me, self.core = steps, me, me % 2
        self.src, self.pair, self.gather, self.inbox, self.full = src, pair, gather, inbox, full
        self.pair_sems, self.chip_sems = pair_sems, chip_sems
        self.half = B // 2
        self.parts = src.shape[1] // B
        self.order = sorted(range(self.parts), key=lambda c: c % (self.parts // self.steps))

    def rows(self, core):
        return pl.ds(pl.multiple_of(core * self.half, self.half), self.half)

    def swap_copy(self, c):
        cols = pl.ds(c * B, B)
        return pltpu.make_async_remote_copy(
            src_ref=self.src.at[self.rows(1 - self.core), cols],
            dst_ref=self.pair.at[:, cols],
            send_sem=self.pair_sems.at[0, c],
            recv_sem=self.pair_sems.at[1, c],
            device_id={"row": self.me ^ 1},
            device_id_type=pl.DeviceIdType.MESH,
        )

    def chip_copy(self, c, step):
        cols = pl.ds(c * B, B)
        turn = (step + c * self.steps // self.parts) % self.steps
        return pltpu.make_async_remote_copy(
            src_ref=self.gather.at[step, :, cols],
            dst_ref=self.inbox.at[step, :, cols],
            send_sem=self.chip_sems.at[0, c, step],
            recv_sem=self.chip_sems.at[1, c, step],
            device_id={"row": self.me ^ (2 << turn)},
            device_id_type=pl.DeviceIdType.MESH,
        )

    def back_copy(self, c, core):
        cols = pl.ds(c * B, B)
        return pltpu.make_async_remote_copy(
            src_ref=self.full.at[self.rows(core), cols],
            dst_ref=self.full.at[self.rows(core), cols],
            send_sem=self.pair_sems.at[2, c],
            recv_sem=self.pair_sems.at[3, c],
            device_id={"row": self.me ^ 1},
            device_id_type=pl.DeviceIdType.MESH,
        )

    def swap(self):
        for c in self.order:
            self.swap_copy(c).start()

    def spread(self):
        for c in self.order:
            cols = pl.ds(c * B, B)
            self.swap_copy(c).wait_recv()
            self.gather[0, :, cols] = self.src[self.rows(self.core), cols] + self.pair[:, cols]
            self.chip_copy(c, 0).start()

    def relay(self):
        for step in range(1, self.steps):
            for c in self.order:
                cols = pl.ds(c * B, B)
                self.chip_copy(c, step - 1).wait_recv()
                self.gather[step, :, cols] = (
                    self.gather[step - 1, :, cols] + self.inbox[step - 1, :, cols]
                )
                self.chip_copy(c, step).start()

    def collect(self):
        last = self.steps - 1
        for c in self.order:
            cols = pl.ds(c * B, B)
            self.chip_copy(c, last).wait_recv()
            self.full[self.rows(self.core), cols] = (
                self.gather[last, :, cols] + self.inbox[last, :, cols]
            )
            self.back_copy(c, self.core).start()

    def end(self):
        for c in range(self.parts):
            self.back_copy(c, 1 - self.core).wait_recv()

    def drain(self):
        for c in range(self.parts):
            self.swap_copy(c).wait_send()
            self.back_copy(c, self.core).wait_send()
            for step in range(self.steps):
                self.chip_copy(c, step).wait_send()


def kernel(
    nrow, ncol, m_hbm, m_v, split_v, g2_v, both_v, p_v,
    q_v, a_v, s1_v, s2_v, sp_v, g1_v, c_v, box1, box2, pair_v, gather_v, inbox_v,
    in_sems, chain_sems, g_sems, sems1, sems2, pair_sems, chip_sems, ready,
):
    me = lax.axis_index("row")
    z = lax.axis_index("col")
    height = m_v.shape[0]
    unit = height // CUTS[-1]
    load_m = pltpu.make_async_copy(m_hbm, m_v, in_sems.at[0])
    load_a = pltpu.make_async_copy(m_hbm.at[:, pl.ds(0, B)], a_v, in_sems.at[1])

    barrier = pltpu.get_barrier_semaphore()
    for i in range(1, nrow):
        pl.semaphore_signal(
            barrier, inc=1, device_id={"row": me ^ i}, device_id_type=pl.DeviceIdType.MESH
        )

    def greet(sem, column):
        pl.semaphore_signal(
            sem, inc=1, device_id={"col": column}, device_id_type=pl.DeviceIdType.MESH
        )

    @pl.when(z > 0)
    def _():
        greet(barrier, z - 1)

    @pl.when(z == 0)
    def _():
        load_a.start()
        for i in range(2, ncol):
            greet(barrier, i)

    load_m.start()

    def enter():
        sends_on = jnp.where(z < ncol - 1, 1, 0)
        far = jnp.where(z > 1, 1, 0)
        pl.semaphore_wait(barrier, nrow - 1 + sends_on + far)

    first = Sum(nrow, me, s1_v, box1, g1_v, sems1)
    second = Sum(nrow, me, s2_v, box2, g2_v, sems2)
    steps = gather_v.shape[0]
    coeffs = PairSum(steps, me, sp_v, pair_v, gather_v, inbox_v, p_v, pair_sems, chip_sems)

    @pl.when(z == 0)
    def _():
        load_a.wait()
        s1_v[...] = mm(a_v[...], a_v[...], ((0,), (0,)))

    enter()

    @pl.when(z > 1)
    def _():
        greet(ready, 0)

    def chain(c):
        block = a_v.at[pl.ds(CUTS[c] * unit, (CUTS[c + 1] - CUTS[c]) * unit)]
        return pltpu.make_async_remote_copy(
            src_ref=block,
            dst_ref=block,
            send_sem=chain_sems.at[0, c],
            recv_sem=chain_sems.at[1, c],
            device_id={"col": lax.rem(z + 1, ncol)},
            device_id_type=pl.DeviceIdType.MESH,
        )

    passes_on = (z > 0) & (z < ncol - 1)

    def forward(*chunks):
        for c in chunks:
            chain(c).wait_recv()
            chain(c).start()

    def hand(which, total, i):
        return pltpu.make_async_remote_copy(
            src_ref=total.box.at[0],
            dst_ref=total.full.at[total.rows(me)],
            send_sem=g_sems.at[2 * which, i],
            recv_sem=g_sems.at[2 * which + 1, 0],
            device_id={"col": i},
            device_id_type=pl.DeviceIdType.MESH,
        )

    def give(which, total):
        def send():
            for i in range(ncol - 1, 0, -1):
                hand(which, total, i).start()

        first.own(me, send)

    @pl.when(z == 0)
    def _():
        for c in range(EARLY):
            chain(c).start()
        first.start()
        first.middle()
        if ncol > 2:
            pl.semaphore_wait(ready, ncol - 2)
        give(0, first)
        first.spread()
        for c in range(EARLY, NEXT):
            chain(c).start()

    @pl.when(passes_on)
    def _():
        forward(*range(EARLY))

    @pl.when(z > 0)
    def _():
        first.own(me, lambda: hand(0, first, 0).wait_recv())
        first.spread()

    def send(*chunks):
        for c in chunks:
            chain(c).start()

    def pass_on(k):
        near, far = NEAR.get(k, ()), FAR.get(k, ())
        starts = START.get(k, ())
        if starts:
            pl.when(z == 0)(lambda: send(*starts))
        if near:
            pl.when(passes_on & (z == 1))(lambda: forward(*near))
        if far:
            pl.when(passes_on & (z > 1))(lambda: forward(*far))

    pass_on(-1)
    first.end()
    first.drain()
    factor_steps(g1_v, c_v, pass_on)

    big = 4 * unit

    @pl.when(z == 0)
    def _():
        for c in range(CUTS[-1] // 4):
            rows = pl.ds(c * big, big)
            q_v[rows] = mm(a_v[rows], g1_v[...], ((1,), (1,)))
        q = q_v[...]
        s2_v[...] = mm(q, q, ((0,), (0,)))
        second.start()
        load_m.wait()
        sp_v[...] = mm(q_v[...], m_v[...], ((0,), (0,)))
        coeffs.swap()
        second.middle()
        give(1, second)
        second.spread()
        coeffs.spread()

    @pl.when(z > 0)
    def _():
        load_m.wait()
        def share():
            second.own(me, lambda: hand(1, second, 0).wait_recv())
            second.spread()

        for c in range(CUTS[-1] // 4):
            if c == LAST:
                share()

            @pl.when(z == ncol - 1)
            def _():
                for i in range(CHUNKS):
                    if 4 * c <= CUTS[i] < 4 * c + 4:
                        chain(i).wait_recv()

            rows = pl.ds(c * big, big)
            q = mm(a_v[rows], g1_v[...], ((1,), (1,)))
            q_v[rows] = q
            term = mm(q, m_v[rows], ((0,), (0,)))
            if c == 0:
                sp_v[...] = term
            else:
                sp_v[...] += term
        coeffs.swap()
        coeffs.spread()

    for c in range(CUTS[-1] // 4):
        rows = pl.ds(c * big, big)
        high, low = halves(q_v[rows])
        split_v[rows] = jnp.concatenate([high, low, high], 1)
    coeffs.relay()
    second.end()
    second.drain()

    factor_steps(g2_v, c_v, lambda k: None)
    both_v[...] = mm(g2_v[...], g2_v[...], ((0,), (0,)))
    coeffs.collect()
    coeffs.end()
    coeffs.drain()

    @pl.when(z == 0)
    def _():
        def given():
            for i in range(1, ncol):
                hand(0, first, i).wait_send()
                hand(1, second, i).wait_send()

        first.own(me, given)

    @pl.when(z < ncol - 1)
    def _():
        for c in range(CHUNKS):
            chain(c).wait_send()


def halves(x):
    high = x.astype(jnp.bfloat16)
    return high, (x - high.astype(jnp.float32)).astype(jnp.bfloat16)


def project_kernel(rows, m_ref, split_ref, g2_ref, both_ref, p_ref, out_hbm, top_hbm, out_v, top_v, back_v, sems):
    height, width = m_ref.shape
    part = height // 8
    scale = math.sqrt(rows)
    on_panel = lax.axis_index("col") == 0
    g2 = g2_ref[...]
    back = mm(both_ref[...], p_ref[...], ((1,), (0,)))
    leading = jnp.where(on_panel, -scale * g2.T, back[:, :B])
    high, low = halves(jnp.concatenate([leading, back[:, B:]], 1))
    back_v[:B] = high
    back_v[B : 2 * B] = high
    back_v[2 * B :] = low

    top_v[...] = mm(g2, p_ref[...], ((1,), (0,))) / scale
    top_store = pltpu.make_async_copy(top_v, top_hbm, sems.at[8])
    top_store.start()

    def store(i):
        block = pl.ds(i * part, part)
        return pltpu.make_async_copy(out_v.at[block], out_hbm.at[block], sems.at[i])

    for i in range(8):
        block = pl.ds(i * part, part)
        change = jnp.dot(
            split_ref[block], back_v[...], preferred_element_type=jnp.float32
        )
        base = m_ref[block]
        out_v[block, :B] = jnp.where(on_panel, 0.0, base[:, :B]) - change[:, :B]
        out_v[block, B:] = base[:, B:] - change[:, B:]
        store(i).start()
    top_store.wait()
    for i in range(8):
        store(i).wait()


def on_device(nrow, ncol, matrix):
    height, width = matrix.shape
    slab = max(8, B // nrow)
    steps = (nrow // 2).bit_length() - 1
    f32 = jnp.float32
    dma = pltpu.SemaphoreType.DMA
    shape = jax.ShapeDtypeStruct
    held, basis, inverse, both, coeffs = pl.pallas_call(
        functools.partial(kernel, nrow, ncol),
        out_shape=(
            shape((height, width), f32), shape((height, 3 * B), jnp.bfloat16),
            shape((B, B), f32), shape((B, B), f32), shape((B, width), f32)
        ),
        in_specs=[pl.BlockSpec(memory_space=pltpu.HBM)],
        out_specs=(pl.BlockSpec(memory_space=pltpu.VMEM),) * 5,
        scratch_shapes=[
            pltpu.VMEM((height, B), f32),
            pltpu.VMEM((height, B), f32),
            pltpu.VMEM((B, B), f32),
            pltpu.VMEM((B, B), f32),
            pltpu.VMEM((B, width), f32),
            pltpu.VMEM((B, B), f32),
            pltpu.VMEM((S * S, B), f32),
            pltpu.VMEM((nrow, slab, B), f32),
            pltpu.VMEM((nrow, slab, B), f32),
            pltpu.VMEM((B // 2, width), f32),
            pltpu.VMEM((steps, B // 2, width), f32),
            pltpu.VMEM((steps, B // 2, width), f32),
            dma((2,)),
            dma((2, CHUNKS)),
            dma((4, ncol)),
            dma((4, nrow)),
            dma((4, nrow)),
            dma((4, width // B)),
            dma((2, width // B, steps)),
            pltpu.SemaphoreType.REGULAR,
        ],
        compiler_params=pltpu.CompilerParams(
            collective_id=0, has_side_effects=True, vmem_limit_bytes=12 * 2**20
        ),
    )(pltpu.with_memory_space_constraint(matrix, pltpu.HBM))
    whole = pl.BlockSpec(memory_space=pltpu.VMEM)
    return pl.pallas_call(
        functools.partial(project_kernel, height * nrow),
        out_shape=(shape((height, width), f32), shape((B, width), f32)),
        in_specs=[whole] * 5,
        out_specs=(pl.BlockSpec(memory_space=pl.ANY),) * 2,
        scratch_shapes=[
            pltpu.VMEM((height, width), f32),
            pltpu.VMEM((B, width), f32),
            pltpu.VMEM((3 * B, width), jnp.bfloat16),
            dma((9,)),
        ],
        compiler_params=pltpu.CompilerParams(vmem_limit_bytes=12 * 2**20),
    )(held, basis, inverse, both, coeffs)


def solution(mesh):
    nrow, ncol = mesh.shape["row"], mesh.shape["col"]
    return jax.shard_map(
        functools.partial(on_device, nrow, ncol),
        mesh=mesh,
        in_specs=(P("row", "col"),),
        out_specs=(P("row", "col"), P(None, "col")),
        check_vma=False,
    )
```
